32 devices in a mesh: seq: 16 (over z, y, core), batch: 2 (over x).
Axes of the slice: x: 2, y: 2, z: 4, core: 2. Of those that a mesh axis runs over, the one named last changes fastest.
Arguments:
- nucleotide_codes: int32 [2, 8192], P('batch', 'seq'), may hold values from 0 to 15
- symbol_vector_lookup: bfloat16 [16, 512], replicated, may hold values from -6 to 6
- normalizer_multipliers: float32 [2, 2, 512], replicated, may hold values from 0.25 to 1.75
- filter_coefficients: bfloat16 [2, 4608, 512], P(None, 'batch'), may hold values from -0.09375 to 0.09375
- triple_head_mappings: bfloat16 [2, 512, 1536], P(None, None, 'batch'), may hold values from -0.25 to 0.25
- attention_final_mixing: bfloat16 [2, 512, 512], P(None, 'batch'), may hold values from -0.25 to 0.25
- logit_divisor_heads: float32 [2, 8], replicated, may hold values from 4 to 160
- permitted_pairs: int32 [2, 64, 25], P(None, 'seq'), may hold values 0 or 1
Outputs:
- encoded: bfloat16 [2, 8192, 512], P('batch', 'seq')
The draws below stay inside these ranges and needn't reach their ends.
All inputs are finite; a program needn't handle non-finite values. No bound on the sum of `permitted_pairs` on one device may be relied on, other than what follows from the above.
Results may differ from the reference program's by a relative error of at most 0.035.
Values may be sent and summed in bfloat16 or wider, within the bound.
A program may use at most 128 MiB of HBM per device.

```python
import math
import jax
import jax.numpy as jnp
import numpy as np
from jax import lax

D = 512
HEADS = 8
HEAD = 64
KERNEL = 9
VOCAB = 16
LAYERS = 2
BLK = 128
WIN = 12
SEQS = 2
LENGTH = 8192
NBLK = 64


def draw_logit_divisor_heads(key, part):
    fraction = jax.random.uniform(key, (LAYERS, HEADS), jnp.float32)
    lower, upper = (4.0, 24.0)
    return jnp.exp(jnp.log(lower) + fraction * (jnp.log(upper) - jnp.log(lower))).astype(jnp.float32)


def set_ends(values, rng, smallest, top_value):
    longest = values.shape.index(max(values.shape))
    spots = []
    for shift in (0, 1):
        where = [jax.random.randint(jax.random.fold_in(rng, axis), (), 0, length) for axis, length in enumerate(values.shape)]
        where[longest] = (where[longest] + shift) % values.shape[longest]
        spots.append(tuple(where))
    return values.at[spots[0]].set(smallest).at[spots[1]].set(top_value)


def levels(stream_key, dims, split, low, high):
    level = 1.0
    for position, blocks in split:
        heights = jax.random.uniform(jax.random.fold_in(jax.random.fold_in(stream_key, 6), position), (blocks,), jnp.float32, low / len(split), high / len(split))
        level = level * jnp.repeat(jnp.exp(heights), dims[position] // blocks).reshape((-1,) + (1,) * (len(dims) - 1 - position))
    return level


def cumulative_ranks(amount, skew):
    portions = [(1 << 20) // math.isqrt(grade ** skew) + 1 for grade in range(1, amount + 1)]
    deviation = 1 + sum(portions) // (1 << 30)
    return np.cumsum(np.array([max(1, weight // deviation) for weight in portions]))


def ranked(own_key, shape, amount, lean):
    listing = cumulative_ranks(amount, lean)
    lot = jax.random.randint(jax.random.fold_in(own_key, 1), shape, 0, int(listing[amount - 1]))
    grade = jnp.searchsorted(jnp.asarray(listing, jnp.int32), lot, side="right")
    return jax.random.permutation(jax.random.fold_in(own_key, 2), amount)[grade].astype(jnp.int32)


def bell_draw(key, extent, deviation, limit, cuts=(), kind=jnp.bfloat16):
    array = deviation * jax.random.normal(key, extent, jnp.float32)
    if cuts:
        array = array * levels(key, extent, cuts, -0.22, 0.18)
    return jnp.clip(array, -limit, limit).astype(kind)


def setup_inputs(seed: int = 0) -> dict:
    key_of = jax.random.split(jax.random.key(seed), 9)
    return {
        "nucleotide_codes": set_ends(ranked(key_of[0], (SEQS, LENGTH), VOCAB, 1), jax.random.fold_in(key_of[0], 3), 0, VOCAB - 1).astype(jnp.int32),
        "symbol_vector_lookup": bell_draw(key_of[1], (VOCAB, D), 1.0, 6.0),
        "normalizer_multipliers": jnp.clip(1.0 + 0.15 * jax.random.normal(key_of[2], (LAYERS, 2, D), jnp.float32), 0.25, 1.75),
        "filter_coefficients": bell_draw(key_of[3], (LAYERS, KERNEL * D, D), (KERNEL * D) ** -0.5, 0.09375, ((1, 2),)),
        "triple_head_mappings": bell_draw(key_of[4], (LAYERS, D, 3 * D), D ** -0.5, 0.25, ((2, 2),)),
        "attention_final_mixing": bell_draw(key_of[5], (LAYERS, D, D), D ** -0.5, 0.25, ((1, 2),)),
        "logit_divisor_heads": draw_logit_divisor_heads(jax.random.fold_in(key_of[8], 71), 0),
        "permitted_pairs": set_ends((jax.random.randint(key_of[7], (LAYERS, NBLK, 2 * WIN + 1), 0, 2) < 1).astype(jnp.int32), jax.random.fold_in(key_of[7], 1), 0, 1),
    }


def norm_rows(stream, gain):
    values = stream.astype(jnp.float32)
    scaled = values * lax.rsqrt(lax.optimization_barrier(jnp.mean(values * values, axis=-1, keepdims=True)) + 1e-06)
    return (scaled * gain).astype(jnp.bfloat16)

def unit_heads(matrix):
    shaped = matrix.reshape(matrix.shape[0], HEADS, HEAD)
    scaled = shaped * lax.rsqrt(lax.optimization_barrier(jnp.mean(shaped * shaped, axis=-1, keepdims=True)) + 1e-06)
    return (scaled / HEAD ** 0.5).astype(jnp.bfloat16)

def attend(query_block, key_window, value_window, valid, logit_multiplier):
    scores = jnp.einsum('qhd,khd->hqk', query_block.astype(jnp.float32), key_window.astype(jnp.float32))
    scores = scores * logit_multiplier[:, None, None]
    scores = jnp.where(valid[None, None, :], scores, -1e+30)
    peak = lax.optimization_barrier(jnp.max(scores, axis=-1, keepdims=True))
    expo = jnp.exp(scores - peak) * valid[None, None, :].astype(jnp.float32)
    weights = (expo / lax.optimization_barrier(jnp.sum(expo, axis=-1, keepdims=True))).astype(jnp.bfloat16)
    result = jnp.einsum('hqk,khd->qhd', weights.astype(jnp.float32), value_window.astype(jnp.float32))
    return result.astype(jnp.bfloat16).reshape(query_block.shape[0], D)

def reference(nucleotide_codes, symbol_vector_lookup, normalizer_multipliers, filter_coefficients, triple_head_mappings, attention_final_mixing, logit_divisor_heads, permitted_pairs):
    reach = WIN * BLK
    span = (2 * WIN + 1) * BLK
    offsets = jnp.arange(-WIN, WIN + 1, dtype=jnp.int32)

    def encode(sequence):
        onehot = (sequence[:, None] == jnp.arange(VOCAB, dtype=jnp.int32)[None, :]).astype(jnp.bfloat16)
        stream = jnp.dot(onehot, symbol_vector_lookup, preferred_element_type=jnp.float32).astype(jnp.bfloat16)
        for transform_stratum in range(LAYERS):
            normed = norm_rows(stream, normalizer_multipliers[transform_stratum, 0])
            padded = jnp.pad(normed, ((KERNEL // 2, KERNEL // 2), (0, 0)))
            unfold = jnp.concatenate([padded[tap:tap + LENGTH] for tap in range(KERNEL)], axis=1)
            conv = jnp.dot(unfold, filter_coefficients[transform_stratum], preferred_element_type=jnp.float32)
            mixed = (stream.astype(jnp.float32) + jax.nn.silu(conv)).astype(jnp.bfloat16)
            inputs = norm_rows(mixed, normalizer_multipliers[transform_stratum, 1])
            proj = jnp.dot(inputs, triple_head_mappings[transform_stratum], preferred_element_type=jnp.float32)
            queries = unit_heads(proj[:, :D])
            keys = unit_heads(proj[:, D:2 * D])
            values = proj[:, 2 * D:].astype(jnp.bfloat16).reshape(LENGTH, HEADS, HEAD)
            keys_padded = jnp.pad(keys, ((reach, reach), (0, 0), (0, 0)))
            values_padded = jnp.pad(values, ((reach, reach), (0, 0), (0, 0)))
            logit_multiplier = logit_divisor_heads[transform_stratum]
            layer_tiles = permitted_pairs[transform_stratum]

            def one_block(index):
                query_block = lax.dynamic_slice_in_dim(queries, index * BLK, BLK, 0)
                key_window = lax.dynamic_slice_in_dim(keys_padded, index * BLK, span, 0)
                value_window = lax.dynamic_slice_in_dim(values_padded, index * BLK, span, 0)
                target = index + offsets
                allowed = (target >= 0) & (target < NBLK) & ((layer_tiles[index] == 1) | (offsets == 0))
                valid = jnp.repeat(allowed, BLK)
                return attend(query_block, key_window, value_window, valid, logit_multiplier)
            attended = lax.map(one_block, jnp.arange(NBLK, dtype=jnp.int32)).reshape(LENGTH, D)
            update = jnp.dot(attended, attention_final_mixing[transform_stratum], preferred_element_type=jnp.float32)
            stream = (mixed.astype(jnp.float32) + update).astype(jnp.bfloat16)
        return stream
    return lax.map(encode, nucleotide_codes)
```

```python
import jax
import jax.numpy as jnp
from jax import lax
from jax.experimental import pallas as pl
from jax.experimental.pallas import tpu as pltpu
from jax.sharding import PartitionSpec as P

HEADS = 8
HEAD = 64
KERNEL = 9
VOCAB = 16
LAYERS = 2
BLK = 128
WIN = 12
D = 512
TILE = 512
GROUP = 4
SLAB = GROUP * HEAD
LOG2E = 1.4426950408889634
F32 = jnp.float32
BF16 = jnp.bfloat16


def shifted(array, axis, by):
    devices = lax.axis_size(axis)
    pairs = [(i, i + by) for i in range(devices) if 0 <= i + by < devices]
    return lax.ppermute(array, axis, pairs)


def extend(block, axis, rims, dim=0):
    below = [shifted(block, axis, d) for d in range(rims, 0, -1)]
    above = [shifted(block, axis, -d) for d in range(1, rims + 1)]
    return jnp.concatenate(below + [block] + above, axis=dim)


def dot(a, b):
    return jnp.dot(a, b, preferred_element_type=F32)


def norm_rows(values, gain):
    scaled = values * lax.rsqrt(jnp.mean(values * values, axis=-1, keepdims=True) + 1e-06)
    return (scaled * gain).astype(BF16)


def unit_heads(p):
    a = lax.broadcasted_iota(jnp.int32, (SLAB, SLAB), 0) // HEAD
    b = lax.broadcasted_iota(jnp.int32, (SLAB, SLAB), 1) // HEAD
    ones = (a == b).astype(F32).astype(BF16)
    parts = []
    for g in range(D // SLAB):
        piece = p[:, g * SLAB : (g + 1) * SLAB]
        square = piece * piece
        high = square.astype(BF16)
        low = (square - high.astype(F32)).astype(BF16)
        total = dot(high, ones) + dot(low, ones)
        scale = lax.rsqrt(total * (1.0 / HEAD) + 1e-06) * (1.0 / HEAD**0.5)
        parts.append((piece * scale).astype(BF16))
    return jnp.concatenate(parts, axis=1)


def dense0_kernel(own, codes_ref, high_ref, low_ref, table_ref, gain_ref, w_ref, k_ref, v_ref, q_ref, mixed_ref):
    vocab = lax.broadcasted_iota(jnp.int32, (VOCAB, TILE), 0)
    hot = [
        (codes_ref[j : j + 1, :] == vocab).astype(F32).astype(BF16) for j in range(KERNEL)
    ]
    dims = (((0,), (0,)), ((), ()))
    stream = lax.dot_general(hot[KERNEL // 2], table_ref[...], dims, preferred_element_type=F32)
    every = jnp.concatenate(hot, axis=0)
    conv = lax.dot_general(every, high_ref[...], dims, preferred_element_type=F32)
    conv += lax.dot_general(every, low_ref[...], dims, preferred_element_type=F32)
    mixed = (stream + conv / (1.0 + jnp.exp(-conv))).astype(BF16)
    inputs = norm_rows(mixed.astype(F32), gain_ref[...])
    k_ref[...] = unit_heads(dot(inputs, w_ref[:, D : 2 * D]))
    v_ref[...] = dot(inputs, w_ref[:, 2 * D :]).astype(BF16)

    @pl.when(pl.program_id(0) == own)
    def _():
        q_ref[...] = unit_heads(dot(inputs, w_ref[:, :D]))
        mixed_ref[...] = mixed


def dense0(codes9, high, low, table, gain, w, own):
    rows = codes9.shape[1]
    whole = lambda shape: pl.BlockSpec(shape, lambda i: (0, 0))
    tile = pl.BlockSpec((TILE, D), lambda i: (i, 0))
    return pl.pallas_call(
        lambda *refs: dense0_kernel(own, *refs),
        grid=(rows // TILE,),
        in_specs=[
            pl.BlockSpec((codes9.shape[0], TILE), lambda i: (0, i)),
            whole(high.shape),
            whole(low.shape),
            whole(table.shape),
            whole(gain.shape),
            whole(w.shape),
        ],
        out_specs=[tile, tile, whole((TILE, D)), whole((TILE, D))],
        out_shape=[jax.ShapeDtypeStruct((rows, D), BF16)] * 2
        + [jax.ShapeDtypeStruct((TILE, D), BF16)] * 2,
        compiler_params=pltpu.CompilerParams(vmem_limit_bytes=40 * 2**20),
        cost_estimate=pl.CostEstimate(
            flops=2 * rows * D * (3 * D), bytes_accessed=4 * rows * D + 2**21, transcendentals=rows * D
        ),
    )(codes9, high, low, table, gain, w)


def project_kernel(own, x_ref, w_ref, k_ref, v_ref, q_ref):
    inputs = x_ref[...]
    k_ref[...] = unit_heads(dot(inputs, w_ref[:, D : 2 * D]))
    v_ref[...] = dot(inputs, w_ref[:, 2 * D :]).astype(BF16)

    @pl.when(pl.program_id(0) == own)
    def _():
        q_ref[...] = unit_heads(dot(inputs, w_ref[:, :D]))


def project(x, w, own):
    rows = x.shape[0]
    whole = lambda shape: pl.BlockSpec(shape, lambda i: (0, 0))
    tile = pl.BlockSpec((TILE, D), lambda i: (i, 0))
    return pl.pallas_call(
        lambda *refs: project_kernel(own, *refs),
        grid=(rows // TILE,),
        in_specs=[tile, whole(w.shape)],
        out_specs=[tile, tile, whole((TILE, D))],
        out_shape=[jax.ShapeDtypeStruct((rows, D), BF16)] * 2
        + [jax.ShapeDtypeStruct((TILE, D), BF16)],
        compiler_params=pltpu.CompilerParams(vmem_limit_bytes=40 * 2**20),
        cost_estimate=pl.CostEstimate(
            flops=2 * rows * D * (2 * D), bytes_accessed=6 * rows * D + 2**21, transcendentals=rows * D
        ),
    )(x, w)


def attention_kernel(
    list_ref, count_ref, mult_ref, q_ref, k_ref, v_ref, mixed_ref, w_ref, out_ref, s_ref, m_ref, l_ref, acc_ref
):
    i = pl.program_id(0)
    count = count_ref[i]
    pairs = (count + 1) // 2
    lane = lax.broadcasted_iota(jnp.int32, (BLK, SLAB), 1) // HEAD
    joined = []

    def chunk(ref, p, g):
        first = pl.multiple_of(list_ref[i, 2 * p] * BLK, BLK)
        second = pl.multiple_of(list_ref[i, 2 * p + 1] * BLK, BLK)
        lanes = slice(g * SLAB, (g + 1) * SLAB)
        return jnp.concatenate([ref[pl.ds(first, BLK), lanes], ref[pl.ds(second, BLK), lanes]], axis=0)

    for g in range(HEADS // GROUP):
        q = q_ref[:, g * SLAB : (g + 1) * SLAB]
        stacked = jnp.concatenate(
            [jnp.where(lane == h, q, jnp.zeros_like(q)) for h in range(GROUP)], axis=0
        )
        m_ref[...] = jnp.full_like(m_ref, -1e30)
        l_ref[...] = jnp.zeros_like(l_ref)
        acc_ref[...] = jnp.zeros_like(acc_ref)

        def score(p, carry):
            s = lax.dot_general(
                stacked, chunk(k_ref, p, g), (((1,), (1,)), ((), ())), preferred_element_type=F32
            )
            bias = jnp.where(2 * p + 1 < count, 0.0, -1e30).astype(F32)
            left, right = s[:, :BLK], s[:, BLK:] + bias
            s_ref[p, :, :BLK] = left
            s_ref[p, :, BLK:] = right
            m_ref[...] = jnp.maximum(m_ref[...], jnp.maximum(left, right))
            return carry

        lax.fori_loop(0, pairs, score, 0)
        for h in range(GROUP):
            rows = slice(h * BLK, (h + 1) * BLK)
            peak = jnp.max(m_ref[rows, :], axis=1, keepdims=True) * mult_ref[g * GROUP + h]
            m_ref[rows, :] = jnp.broadcast_to(peak, (BLK, BLK))

        def weigh(p, carry):
            probs = []
            for h in range(GROUP):
                rows = slice(h * BLK, (h + 1) * BLK)
                mult = mult_ref[g * GROUP + h]
                peak = m_ref[rows, :]
                left = jnp.exp2(s_ref[p, rows, :BLK] * mult - peak)
                right = jnp.exp2(s_ref[p, rows, BLK:] * mult - peak)
                l_ref[rows, :] += left + right
                probs.append(jnp.concatenate([left.astype(BF16), right.astype(BF16)], axis=1))
            acc_ref[...] += dot(jnp.concatenate(probs, axis=0), chunk(v_ref, p, g))
            return carry

        lax.fori_loop(0, pairs, weigh, 0)
        result = jnp.zeros((BLK, SLAB), F32)
        for h in range(GROUP):
            rows = slice(h * BLK, (h + 1) * BLK)
            total = jnp.sum(l_ref[rows, :], axis=1, keepdims=True)
            result = jnp.where(lane == h, acc_ref[rows, :] * (1.0 / total), result)
        joined.append(result.astype(BF16))
    update = dot(jnp.concatenate(joined, axis=1), w_ref[...])
    out_ref[...] = (mixed_ref[...].astype(F32) + update).astype(BF16)


def attention(lists, counts, mult, q, k, v, mixed, w):
    rows = q.shape[0]
    whole = lambda shape: pl.BlockSpec(shape, lambda i, *_: (0, 0))
    tile = pl.BlockSpec((BLK, D), lambda i, *_: (i, 0))
    half = (2 * WIN + 2) // 2
    return pl.pallas_call(
        attention_kernel,
        grid_spec=pltpu.PrefetchScalarGridSpec(
            num_scalar_prefetch=3,
            grid=(rows // BLK,),
            in_specs=[tile, whole(k.shape), whole(v.shape), tile, whole(w.shape)],
            out_specs=tile,
            scratch_shapes=[
                pltpu.VMEM((half, GROUP * BLK, 2 * BLK), F32),
                pltpu.VMEM((GROUP * BLK, BLK), F32),
                pltpu.VMEM((GROUP * BLK, BLK), F32),
                pltpu.VMEM((GROUP * BLK, SLAB), F32),
            ],
        ),
        out_shape=jax.ShapeDtypeStruct((rows, D), BF16),
        compiler_params=pltpu.CompilerParams(vmem_limit_bytes=48 * 2**20),
        cost_estimate=pl.CostEstimate(
            flops=16 * 10**9, bytes_accessed=8 * 2**20, transcendentals=rows * HEADS * 13 * BLK
        ),
    )(lists, counts, mult, q, k, v, mixed, w)


def tap_products(table, gain, taps):
    held = taps.shape[0]
    devices = lax.axis_size("batch")
    me = lax.axis_index("batch")
    spans = [(-(-(b + 1) * held // D)) - b * held // D for b in range(devices)]
    span = min(KERNEL, max(spans))

    def first(b):
        return jnp.minimum(b * held // D, KERNEL - span)

    normed = norm_rows(table.astype(F32), gain)
    begin = me * held
    copies = -(-held // D) + 1
    columns = lax.dynamic_slice_in_dim(jnp.tile(normed, (1, copies)), begin % D, held, 1)
    tap = (begin + jnp.arange(held, dtype=jnp.int32)) // D - first(me)
    mask = tap[None, :] == jnp.arange(span, dtype=jnp.int32)[:, None]
    spread = jnp.where(mask[:, None, :], columns[None], jnp.zeros((), BF16)).reshape(span * VOCAB, held)
    part = dot(spread, taps)
    total = jnp.zeros((KERNEL * VOCAB, D), F32)
    for step in range(devices):
        if step == 0:
            piece = part
        else:
            piece = lax.ppermute(part, "batch", [(b, (b + step) % devices) for b in range(devices)])
        place = first((me - step) % devices) * VOCAB
        total += lax.dynamic_update_slice_in_dim(jnp.zeros_like(total), piece, place, 0)
    return total


def local(codes, table, gains, taps, qkv, mixing, divisors, permitted):
    rows = codes.shape[1]
    rims = -(-WIN * BLK // rows)
    blocks = rows // BLK
    first_block = lax.axis_index("seq") * blocks
    total_blocks = blocks * lax.axis_size("seq")

    offsets = jnp.arange(-WIN, WIN + 1, dtype=jnp.int32)
    index = jnp.arange(blocks, dtype=jnp.int32)[:, None]
    target = first_block + index + offsets[None, :]
    allowed = (target >= 0) & (target < total_blocks)
    allowed = allowed[None] & ((permitted == 1) | (offsets == 0)[None, None])
    counts = jnp.sum(allowed.astype(jnp.int32), axis=-1)
    order = jnp.arange(2 * WIN + 1)
    place = jnp.sum(
        (allowed[:, :, None, :] & (order[None, :] < order[:, None])[None, None]).astype(jnp.int32), axis=-1
    )
    slots = jnp.arange(2 * WIN + 2, dtype=jnp.int32)
    picked = allowed[:, :, None, :] & (place[:, :, None, :] == slots[None, None, :, None])
    window = index + offsets[None, :] + rims * blocks
    lists = jnp.sum(jnp.where(picked, window[None, :, None, :], 0), axis=-1)
    mult = divisors * LOG2E

    wide = extend(codes[0] + 1, "seq", rims + 1) - 1
    begin = rows - KERNEL // 2
    span = (2 * rims + 1) * rows
    codes9 = jnp.stack([wide[begin + j : begin + j + span] for j in range(KERNEL)] + [wide[:span]] * (16 - KERNEL))
    products = tap_products(table, gains[0, 0], taps[0])
    high = products.astype(BF16)
    low = (products - high.astype(F32)).astype(BF16)
    w0 = lax.all_gather(qkv[0], "batch", axis=1, tiled=True)
    k, v, q, mixed = dense0(codes9, high, low, table, gains[0, 1][None], w0, rims)
    out0 = lax.all_gather(mixing[0], "batch", axis=0, tiled=True)
    stream = attention(lists[0], counts[0], mult[0], q, k, v, mixed, out0)

    taps1 = lax.all_gather(taps[1], "batch", axis=0, tiled=True)
    w1 = lax.all_gather(qkv[1], "batch", axis=1, tiled=True)
    out1 = lax.all_gather(mixing[1], "batch", axis=0, tiled=True)
    half = KERNEL // 2
    normed = norm_rows(stream.astype(F32), gains[1, 0])
    below = shifted(normed[rows - half :], "seq", 1)
    above = shifted(normed[:half], "seq", -1)
    padded = jnp.concatenate([below, normed, above], axis=0)
    unfold = jnp.concatenate([padded[j : j + rows] for j in range(KERNEL)], axis=1)
    conv = dot(unfold, taps1)
    mixed = (stream.astype(F32) + jax.nn.silu(conv)).astype(BF16)
    inputs = norm_rows(mixed.astype(F32), gains[1, 1])
    k, v, q = project(extend(inputs, "seq", rims), w1, rims)
    return attention(lists[1], counts[1], mult[1], q, k, v, mixed, out1)[None]


def solution(mesh):
    in_specs = (
        P("batch", "seq"),
        P(),
        P(),
        P(None, "batch", None),
        P(None, None, "batch"),
        P(None, "batch", None),
        P(),
        P(None, "seq", None),
    )
    out_specs = P("batch", "seq", None)
    return jax.shard_map(local, mesh=mesh, in_specs=in_specs, out_specs=out_specs, check_vma=False)
```

```python
import jax
import jax.numpy as jnp
from jax import lax
from jax.experimental import pallas as pl
from jax.experimental.pallas import tpu as pltpu
from jax.sharding import PartitionSpec as P

HEADS = 8
HEAD = 64
KERNEL = 9
VOCAB = 16
LAYERS = 2
BLK = 128
WIN = 12
D = 512
TILE = 512
GROUP = 4
SLAB = GROUP * HEAD
LOG2E = 1.4426950408889634
F32 = jnp.float32
BF16 = jnp.bfloat16


def shifted(array, axis, by):
    devices = lax.axis_size(axis)
    pairs = [(i, i + by) for i in range(devices) if 0 <= i + by < devices]
    return lax.ppermute(array, axis, pairs)


def extend(block, axis, rims, dim=0):
    below = [shifted(block, axis, d) for d in range(rims, 0, -1)]
    above = [shifted(block, axis, -d) for d in range(1, rims + 1)]
    return jnp.concatenate(below + [block] + above, axis=dim)


def dot(a, b):
    return jnp.dot(a, b, preferred_element_type=F32)


def norm_rows(values, gain):
    scaled = values * lax.rsqrt(jnp.mean(values * values, axis=-1, keepdims=True) + 1e-06)
    return (scaled * gain).astype(BF16)


def unit_heads(p):
    a = lax.broadcasted_iota(jnp.int32, (SLAB, SLAB), 0) // HEAD
    b = lax.broadcasted_iota(jnp.int32, (SLAB, SLAB), 1) // HEAD
    ones = (a == b).astype(F32).astype(BF16)
    parts = []
    for g in range(D // SLAB):
        piece = p[:, g * SLAB : (g + 1) * SLAB]
        square = piece * piece
        high = square.astype(BF16)
        low = (square - high.astype(F32)).astype(BF16)
        total = dot(high, ones) + dot(low, ones)
        scale = lax.rsqrt(total * (1.0 / HEAD) + 1e-06) * (1.0 / HEAD**0.5)
        parts.append((piece * scale).astype(BF16))
    return jnp.concatenate(parts, axis=1)


def dense0_kernel(own, codes_ref, high_ref, low_ref, table_ref, gain_ref, w_ref, k_ref, v_ref, q_ref, mixed_ref):
    vocab = lax.broadcasted_iota(jnp.int32, (VOCAB, TILE), 0)
    hot = [
        (codes_ref[j : j + 1, :] == vocab).astype(F32).astype(BF16) for j in range(KERNEL)
    ]
    dims = (((0,), (0,)), ((), ()))
    stream = lax.dot_general(hot[KERNEL // 2], table_ref[...], dims, preferred_element_type=F32)
    every = jnp.concatenate(hot, axis=0)
    conv = lax.dot_general(every, high_ref[...], dims, preferred_element_type=F32)
    conv += lax.dot_general(every, low_ref[...], dims, preferred_element_type=F32)
    mixed = (stream + conv / (1.0 + jnp.exp(-conv))).astype(BF16)
    inputs = norm_rows(mixed.astype(F32), gain_ref[...])
    k_ref[...] = unit_heads(dot(inputs, w_ref[:, D : 2 * D]))
    v_ref[...] = dot(inputs, w_ref[:, 2 * D :]).astype(BF16)

    @pl.when(pl.program_id(0) == own)
    def _():
        q_ref[...] = unit_heads(dot(inputs, w_ref[:, :D]))
        mixed_ref[...] = mixed


def dense0(codes9, high, low, table, gain, w, own):
    rows = codes9.shape[1]
    whole = lambda shape: pl.BlockSpec(shape, lambda i: (0, 0))
    tile = pl.BlockSpec((TILE, D), lambda i: (i, 0))
    return pl.pallas_call(
        lambda *refs: dense0_kernel(own, *refs),
        grid=(rows // TILE,),
        in_specs=[
            pl.BlockSpec((codes9.shape[0], TILE), lambda i: (0, i)),
            whole(high.shape),
            whole(low.shape),
            whole(table.shape),
            whole(gain.shape),
            whole(w.shape),
        ],
        out_specs=[tile, tile, whole((TILE, D)), whole((TILE, D))],
        out_shape=[jax.ShapeDtypeStruct((rows, D), BF16)] * 2
        + [jax.ShapeDtypeStruct((TILE, D), BF16)] * 2,
        compiler_params=pltpu.CompilerParams(vmem_limit_bytes=40 * 2**20),
        cost_estimate=pl.CostEstimate(
            flops=2 * rows * D * (3 * D), bytes_accessed=4 * rows * D + 2**21, transcendentals=rows * D
        ),
    )(codes9, high, low, table, gain, w)


def project_kernel(own, x_ref, w_ref, k_ref, v_ref, q_ref):
    inputs = x_ref[...]
    k_ref[...] = unit_heads(dot(inputs, w_ref[:, D : 2 * D]))
    v_ref[...] = dot(inputs, w_ref[:, 2 * D :]).astype(BF16)

    @pl.when(pl.program_id(0) == own)
    def _():
        q_ref[...] = unit_heads(dot(inputs, w_ref[:, :D]))


def project(x, w, own):
    rows = x.shape[0]
    whole = lambda shape: pl.BlockSpec(shape, lambda i: (0, 0))
    tile = pl.BlockSpec((TILE, D), lambda i: (i, 0))
    return pl.pallas_call(
        lambda *refs: project_kernel(own, *refs),
        grid=(rows // TILE,),
        in_specs=[tile, whole(w.shape)],
        out_specs=[tile, tile, whole((TILE, D))],
        out_shape=[jax.ShapeDtypeStruct((rows, D), BF16)] * 2
        + [jax.ShapeDtypeStruct((TILE, D), BF16)],
        compiler_params=pltpu.CompilerParams(vmem_limit_bytes=40 * 2**20),
        cost_estimate=pl.CostEstimate(
            flops=2 * rows * D * (2 * D), bytes_accessed=6 * rows * D + 2**21, transcendentals=rows * D
        ),
    )(x, w)


def attention_kernel(
    list_ref, count_ref, mult_ref, q_ref, k_ref, v_ref, mixed_ref, w_ref, out_ref, s_ref, m_ref, l_ref, acc_ref
):
    i = pl.program_id(0)
    count = count_ref[i]
    pairs = (count + 1) // 2
    lane = lax.broadcasted_iota(jnp.int32, (BLK, SLAB), 1) // HEAD
    joined = []

    def chunk(ref, p, g):
        first = pl.multiple_of(list_ref[i, 2 * p] * BLK, BLK)
        second = pl.multiple_of(list_ref[i, 2 * p + 1] * BLK, BLK)
        lanes = slice(g * SLAB, (g + 1) * SLAB)
        return jnp.concatenate([ref[pl.ds(first, BLK), lanes], ref[pl.ds(second, BLK), lanes]], axis=0)

    for g in range(HEADS // GROUP):
        q = q_ref[:, g * SLAB : (g + 1) * SLAB]
        stacked = jnp.concatenate(
            [jnp.where(lane == h, q, jnp.zeros_like(q)) for h in range(GROUP)], axis=0
        )
        m_ref[...] = jnp.full_like(m_ref, -1e30)
        l_ref[...] = jnp.zeros_like(l_ref)
        acc_ref[...] = jnp.zeros_like(acc_ref)

        def score(p, carry):
            s = lax.dot_general(
                stacked, chunk(k_ref, p, g), (((1,), (1,)), ((), ())), preferred_element_type=F32
            )
            bias = jnp.where(2 * p + 1 < count, 0.0, -1e30).astype(F32)
            left, right = s[:, :BLK], s[:, BLK:] + bias
            s_ref[p, :, :BLK] = left
            s_ref[p, :, BLK:] = right
            m_ref[...] = jnp.maximum(m_ref[...], jnp.maximum(left, right))
            return carry

        lax.fori_loop(0, pairs, score, 0)
        for h in range(GROUP):
            rows = slice(h * BLK, (h + 1) * BLK)
            peak = jnp.max(m_ref[rows, :], axis=1, keepdims=True) * mult_ref[g * GROUP + h]
            m_ref[rows, :] = jnp.broadcast_to(peak, (BLK, BLK))

        def weigh(p, carry):
            probs = []
            for h in range(GROUP):
                rows = slice(h * BLK, (h + 1) * BLK)
                mult = mult_ref[g * GROUP + h]
                peak = m_ref[rows, :]
                left = jnp.exp2(s_ref[p, rows, :BLK] * mult - peak)
                right = jnp.exp2(s_ref[p, rows, BLK:] * mult - peak)
                l_ref[rows, :] += left + right
                probs.append(jnp.concatenate([left.astype(BF16), right.astype(BF16)], axis=1))
            acc_ref[...] += dot(jnp.concatenate(probs, axis=0), chunk(v_ref, p, g))
            return carry

        lax.fori_loop(0, pairs, weigh, 0)
        result = jnp.zeros((BLK, SLAB), F32)
        for h in range(GROUP):
            rows = slice(h * BLK, (h + 1) * BLK)
            total = jnp.sum(l_ref[rows, :], axis=1, keepdims=True)
            result = jnp.where(lane == h, acc_ref[rows, :] * (1.0 / total), result)
        joined.append(result.astype(BF16))
    update = dot(jnp.concatenate(joined, axis=1), w_ref[...])
    out_ref[...] = (mixed_ref[...].astype(F32) + update).astype(BF16)


def attention(lists, counts, mult, q, k, v, mixed, w):
    rows = q.shape[0]
    whole = lambda shape: pl.BlockSpec(shape, lambda i, *_: (0, 0))
    tile = pl.BlockSpec((BLK, D), lambda i, *_: (i, 0))
    half = (2 * WIN + 2) // 2
    return pl.pallas_call(
        attention_kernel,
        grid_spec=pltpu.PrefetchScalarGridSpec(
            num_scalar_prefetch=3,
            grid=(rows // BLK,),
            in_specs=[tile, whole(k.shape), whole(v.shape), tile, whole(w.shape)],
            out_specs=tile,
            scratch_shapes=[
                pltpu.VMEM((half, GROUP * BLK, 2 * BLK), F32),
                pltpu.VMEM((GROUP * BLK, BLK), F32),
                pltpu.VMEM((GROUP * BLK, BLK), F32),
                pltpu.VMEM((GROUP * BLK, SLAB), F32),
            ],
        ),
        out_shape=jax.ShapeDtypeStruct((rows, D), BF16),
        compiler_params=pltpu.CompilerParams(vmem_limit_bytes=48 * 2**20),
        cost_estimate=pl.CostEstimate(
            flops=16 * 10**9, bytes_accessed=8 * 2**20, transcendentals=rows * HEADS * 13 * BLK
        ),
    )(lists, counts, mult, q, k, v, mixed, w)


def tap_products(table, gain, taps):
    held = taps.shape[0]
    devices = lax.axis_size("batch")
    me = lax.axis_index("batch")
    spans = [(-(-(b + 1) * held // D)) - b * held // D for b in range(devices)]
    span = min(KERNEL, max(spans))

    def first(b):
        return jnp.minimum(b * held // D, KERNEL - span)

    normed = norm_rows(table.astype(F32), gain)
    begin = me * held
    copies = -(-held // D) + 1
    columns = lax.dynamic_slice_in_dim(jnp.tile(normed, (1, copies)), begin % D, held, 1)
    tap = (begin + jnp.arange(held, dtype=jnp.int32)) // D - first(me)
    mask = tap[None, :] == jnp.arange(span, dtype=jnp.int32)[:, None]
    spread = jnp.where(mask[:, None, :], columns[None], jnp.zeros((), BF16)).reshape(span * VOCAB, held)
    part = dot(spread, taps)
    total = jnp.zeros((KERNEL * VOCAB, D), F32)
    for step in range(devices):
        if step == 0:
            piece = part
        else:
            piece = lax.ppermute(part, "batch", [(b, (b + step) % devices) for b in range(devices)])
        place = first((me - step) % devices) * VOCAB
        total += lax.dynamic_update_slice_in_dim(jnp.zeros_like(total), piece, place, 0)
    return total


def local(codes, table, gains, taps, qkv, mixing, divisors, permitted):
    rows = codes.shape[1]
    rims = -(-WIN * BLK // rows)
    blocks = rows // BLK
    first_block = lax.axis_index("seq") * blocks
    total_blocks = blocks * lax.axis_size("seq")

    offsets = jnp.arange(-WIN, WIN + 1, dtype=jnp.int32)
    index = jnp.arange(blocks, dtype=jnp.int32)[:, None]
    target = first_block + index + offsets[None, :]
    allowed = (target >= 0) & (target < total_blocks)
    allowed = allowed[None] & ((permitted == 1) | (offsets == 0)[None, None])
    counts = jnp.sum(allowed.astype(jnp.int32), axis=-1)
    order = jnp.arange(2 * WIN + 1)
    place = jnp.sum(
        (allowed[:, :, None, :] & (order[None, :] < order[:, None])[None, None]).astype(jnp.int32), axis=-1
    )
    slots = jnp.arange(2 * WIN + 2, dtype=jnp.int32)
    picked = allowed[:, :, None, :] & (place[:, :, None, :] == slots[None, None, :, None])
    window = index + offsets[None, :] + rims * blocks
    lists = jnp.sum(jnp.where(picked, window[None, :, None, :], 0), axis=-1)
    mult = divisors * LOG2E

    margin = (rims + 1) * rows
    every = jnp.pad(lax.all_gather(codes[0], "seq", axis=0, tiled=True), (margin, margin), constant_values=-1)
    wide = lax.dynamic_slice_in_dim(every, lax.axis_index("seq") * rows, 2 * margin + rows, 0)
    begin = rows - KERNEL // 2
    span = (2 * rims + 1) * rows
    codes9 = jnp.stack([wide[begin + j : begin + j + span] for j in range(KERNEL)] + [wide[:span]] * (16 - KERNEL))
    products = tap_products(table, gains[0, 0], taps[0])
    high = products.astype(BF16)
    low = (products - high.astype(F32)).astype(BF16)
    w0 = lax.all_gather(qkv[0], "batch", axis=1, tiled=True)
    k, v, q, mixed = dense0(codes9, high, low, table, gains[0, 1][None], w0, rims)
    out0 = lax.all_gather(mixing[0], "batch", axis=0, tiled=True)
    stream = attention(lists[0], counts[0], mult[0], q, k, v, mixed, out0)

    taps1 = lax.all_gather(taps[1], "batch", axis=0, tiled=True)
    w1 = lax.all_gather(qkv[1], "batch", axis=1, tiled=True)
    out1 = lax.all_gather(mixing[1], "batch", axis=0, tiled=True)
    half = KERNEL // 2
    normed = norm_rows(stream.astype(F32), gains[1, 0])
    below = shifted(normed[rows - half :], "seq", 1)
    above = shifted(normed[:half], "seq", -1)
    padded = jnp.concatenate([below, normed, above], axis=0)
    unfold = jnp.concatenate([padded[j : j + rows] for j in range(KERNEL)], axis=1)
    conv = dot(unfold, taps1)
    mixed = (stream.astype(F32) + jax.nn.silu(conv)).astype(BF16)
    inputs = norm_rows(mixed.astype(F32), gains[1, 1])
    k, v, q = project(extend(inputs, "seq", rims), w1, rims)
    return attention(lists[1], counts[1], mult[1], q, k, v, mixed, out1)[None]


def solution(mesh):
    in_specs = (
        P("batch", "seq"),
        P(),
        P(),
        P(None, "batch", None),
        P(None, None, "batch"),
        P(None, "batch", None),
        P(),
        P(None, "seq", None),
    )
    out_specs = P("batch", "seq", None)
    return jax.shard_map(local, mesh=mesh, in_specs=in_specs, out_specs=out_specs, check_vma=False)
```

```python
import jax
import jax.numpy as jnp
from jax import lax
from jax.experimental import pallas as pl
from jax.experimental.pallas import tpu as pltpu
from jax.sharding import PartitionSpec as P

HEADS = 8
HEAD = 64
KERNEL = 9
VOCAB = 16
LAYERS = 2
BLK = 128
WIN = 12
D = 512
TILE = 512
GROUP = 4
SLAB = GROUP * HEAD
LOG2E = 1.4426950408889634
NARROW = 88.0
F32 = jnp.float32
BF16 = jnp.bfloat16


def shifted(array, axis, by):
    devices = lax.axis_size(axis)
    pairs = [(i, i + by) for i in range(devices) if 0 <= i + by < devices]
    return lax.ppermute(array, axis, pairs)


def extend(block, axis, rims, dim=0):
    below = [shifted(block, axis, d) for d in range(rims, 0, -1)]
    above = [shifted(block, axis, -d) for d in range(1, rims + 1)]
    return jnp.concatenate(below + [block] + above, axis=dim)


def dot(a, b):
    return jnp.dot(a, b, preferred_element_type=F32)


def norm_rows(values, gain):
    scaled = values * lax.rsqrt(jnp.mean(values * values, axis=-1, keepdims=True) + 1e-06)
    return (scaled * gain).astype(BF16)


def unit_heads(p):
    a = lax.broadcasted_iota(jnp.int32, (SLAB, SLAB), 0) // HEAD
    b = lax.broadcasted_iota(jnp.int32, (SLAB, SLAB), 1) // HEAD
    ones = (a == b).astype(F32).astype(BF16)
    parts = []
    for g in range(D // SLAB):
        piece = p[:, g * SLAB : (g + 1) * SLAB]
        square = piece * piece
        high = square.astype(BF16)
        low = (square - high.astype(F32)).astype(BF16)
        total = dot(high, ones) + dot(low, ones)
        scale = lax.rsqrt(total * (1.0 / HEAD) + 1e-06) * (1.0 / HEAD**0.5)
        parts.append((piece * scale).astype(BF16))
    return jnp.concatenate(parts, axis=1)


def dense0_kernel(own, codes_ref, high_ref, low_ref, table_ref, gain_ref, w_ref, k_ref, v_ref, q_ref, mixed_ref):
    vocab = lax.broadcasted_iota(jnp.int32, (VOCAB, TILE), 0)
    hot = [
        (codes_ref[j : j + 1, :] == vocab).astype(F32).astype(BF16) for j in range(KERNEL)
    ]
    dims = (((0,), (0,)), ((), ()))
    stream = lax.dot_general(hot[KERNEL // 2], table_ref[...], dims, preferred_element_type=F32)
    every = jnp.concatenate(hot, axis=0)
    conv = lax.dot_general(every, high_ref[...], dims, preferred_element_type=F32)
    conv += lax.dot_general(every, low_ref[...], dims, preferred_element_type=F32)
    mixed = (stream + conv / (1.0 + jnp.exp(-conv))).astype(BF16)
    inputs = norm_rows(mixed.astype(F32), gain_ref[...])
    k_ref[...] = unit_heads(dot(inputs, w_ref[:, D : 2 * D]))
    v_ref[...] = dot(inputs, w_ref[:, 2 * D :]).astype(BF16)

    @pl.when(pl.program_id(0) == own)
    def _():
        q_ref[...] = unit_heads(dot(inputs, w_ref[:, :D]))
        mixed_ref[...] = mixed


def dense0(codes9, high, low, table, gain, w, own):
    rows = codes9.shape[1]
    whole = lambda shape: pl.BlockSpec(shape, lambda i: (0, 0))
    tile = pl.BlockSpec((TILE, D), lambda i: (i, 0))
    return pl.pallas_call(
        lambda *refs: dense0_kernel(own, *refs),
        grid=(rows // TILE,),
        in_specs=[
            pl.BlockSpec((codes9.shape[0], TILE), lambda i: (0, i)),
            whole(high.shape),
            whole(low.shape),
            whole(table.shape),
            whole(gain.shape),
            whole(w.shape),
        ],
        out_specs=[tile, tile, whole((TILE, D)), whole((TILE, D))],
        out_shape=[jax.ShapeDtypeStruct((rows, D), BF16)] * 2
        + [jax.ShapeDtypeStruct((TILE, D), BF16)] * 2,
        compiler_params=pltpu.CompilerParams(vmem_limit_bytes=40 * 2**20),
        cost_estimate=pl.CostEstimate(
            flops=2 * rows * D * (3 * D), bytes_accessed=4 * rows * D + 2**21, transcendentals=rows * D
        ),
    )(codes9, high, low, table, gain, w)


def project_kernel(own, x_ref, w_ref, k_ref, v_ref, q_ref):
    inputs = x_ref[...]
    k_ref[...] = unit_heads(dot(inputs, w_ref[:, D : 2 * D]))
    v_ref[...] = dot(inputs, w_ref[:, 2 * D :]).astype(BF16)

    @pl.when(pl.program_id(0) == own)
    def _():
        q_ref[...] = unit_heads(dot(inputs, w_ref[:, :D]))


def project(x, w, own):
    rows = x.shape[0]
    whole = lambda shape: pl.BlockSpec(shape, lambda i: (0, 0))
    tile = pl.BlockSpec((TILE, D), lambda i: (i, 0))
    return pl.pallas_call(
        lambda *refs: project_kernel(own, *refs),
        grid=(rows // TILE,),
        in_specs=[tile, whole(w.shape)],
        out_specs=[tile, tile, whole((TILE, D))],
        out_shape=[jax.ShapeDtypeStruct((rows, D), BF16)] * 2
        + [jax.ShapeDtypeStruct((TILE, D), BF16)],
        compiler_params=pltpu.CompilerParams(vmem_limit_bytes=40 * 2**20),
        cost_estimate=pl.CostEstimate(
            flops=2 * rows * D * (2 * D), bytes_accessed=6 * rows * D + 2**21, transcendentals=rows * D
        ),
    )(x, w)


def attention_kernel(
    list_ref, count_ref, mult_ref, q_ref, k_ref, v_ref, mixed_ref, w_ref, out_ref, s_ref, m_ref, l_ref, acc_ref
):
    i = pl.program_id(0)
    count = count_ref[i]
    pairs = (count + 1) // 2
    lane = lax.broadcasted_iota(jnp.int32, (BLK, SLAB), 1) // HEAD
    joined = []

    def chunk(ref, p, g):
        first = pl.multiple_of(list_ref[i, 2 * p] * BLK, BLK)
        second = pl.multiple_of(list_ref[i, 2 * p + 1] * BLK, BLK)
        lanes = slice(g * SLAB, (g + 1) * SLAB)
        return jnp.concatenate([ref[pl.ds(first, BLK), lanes], ref[pl.ds(second, BLK), lanes]], axis=0)

    def gathered(ref, base, blocks, g):
        lanes = slice(g * SLAB, (g + 1) * SLAB)
        starts = [pl.multiple_of(list_ref[i, base + n] * BLK, BLK) for n in range(blocks)]
        return jnp.concatenate([ref[pl.ds(start, BLK), lanes] for start in starts], axis=0)

    for g in range(HEADS // GROUP):
        q = q_ref[:, g * SLAB : (g + 1) * SLAB]
        stacked = jnp.concatenate(
            [jnp.where(lane == h, q, jnp.zeros_like(q)) for h in range(GROUP)], axis=0
        )
        l_ref[...] = jnp.zeros_like(l_ref)
        acc_ref[...] = jnp.zeros_like(acc_ref)
        mults = [mult_ref[g * GROUP + h] for h in range(GROUP)]
        narrow = jnp.maximum(jnp.maximum(mults[0], mults[1]), jnp.maximum(mults[2], mults[3])) <= NARROW

        @pl.when(narrow)
        def _(g=g, stacked=stacked, mults=mults):
            def step(base, blocks, masked):
                keys, values = gathered(k_ref, base, blocks, g), gathered(v_ref, base, blocks, g)
                s = lax.dot_general(stacked, keys, (((1,), (1,)), ((), ())), preferred_element_type=F32)
                probs = []
                for h in range(GROUP):
                    rows = slice(h * BLK, (h + 1) * BLK)
                    scaled = s[rows] * mults[h]
                    if masked:
                        bias = jnp.where(base + 1 < count, 0.0, -1e30).astype(F32)
                        scaled = jnp.concatenate([scaled[:, :BLK], scaled[:, BLK:] + bias], axis=1)
                    expo = jnp.exp2(scaled)
                    part = expo[:, :BLK]
                    for n in range(1, blocks):
                        part += expo[:, n * BLK : (n + 1) * BLK]
                    l_ref[rows, :] += part
                    probs.append(expo.astype(BF16))
                acc_ref[...] += dot(jnp.concatenate(probs, axis=0), values)

            quads = count // 4
            lax.fori_loop(0, quads, lambda p, c: (step(4 * p, 4, False), c)[1], 0)
            rest = (count - 4 * quads + 1) // 2
            lax.fori_loop(0, rest, lambda p, c: (step(4 * quads + 2 * p, 2, True), c)[1], 0)

        @pl.when(jnp.logical_not(narrow))
        def _(g=g, stacked=stacked):
            m_ref[...] = jnp.full_like(m_ref, -1e30)

            def score(p, carry):
                s = lax.dot_general(
                    stacked, chunk(k_ref, p, g), (((1,), (1,)), ((), ())), preferred_element_type=F32
                )
                bias = jnp.where(2 * p + 1 < count, 0.0, -1e30).astype(F32)
                left, right = s[:, :BLK], s[:, BLK:] + bias
                s_ref[p, :, :BLK] = left
                s_ref[p, :, BLK:] = right
                m_ref[...] = jnp.maximum(m_ref[...], jnp.maximum(left, right))
                return carry

            lax.fori_loop(0, pairs, score, 0)
            for h in range(GROUP):
                rows = slice(h * BLK, (h + 1) * BLK)
                peak = jnp.max(m_ref[rows, :], axis=1, keepdims=True) * mult_ref[g * GROUP + h]
                m_ref[rows, :] = jnp.broadcast_to(peak, (BLK, BLK))

            def weigh(p, carry):
                probs = []
                for h in range(GROUP):
                    rows = slice(h * BLK, (h + 1) * BLK)
                    mult = mult_ref[g * GROUP + h]
                    peak = m_ref[rows, :]
                    left = jnp.exp2(s_ref[p, rows, :BLK] * mult - peak)
                    right = jnp.exp2(s_ref[p, rows, BLK:] * mult - peak)
                    l_ref[rows, :] += left + right
                    probs.append(jnp.concatenate([left.astype(BF16), right.astype(BF16)], axis=1))
                acc_ref[...] += dot(jnp.concatenate(probs, axis=0), chunk(v_ref, p, g))
                return carry

            lax.fori_loop(0, pairs, weigh, 0)
        result = jnp.zeros((BLK, SLAB), F32)
        for h in range(GROUP):
            rows = slice(h * BLK, (h + 1) * BLK)
            total = jnp.sum(l_ref[rows, :], axis=1, keepdims=True)
            result = jnp.where(lane == h, acc_ref[rows, :] * (1.0 / total), result)
        joined.append(result.astype(BF16))
    update = dot(jnp.concatenate(joined, axis=1), w_ref[...])
    out_ref[...] = (mixed_ref[...].astype(F32) + update).astype(BF16)


def attention(lists, counts, mult, q, k, v, mixed, w):
    rows = q.shape[0]
    whole = lambda shape: pl.BlockSpec(shape, lambda i, *_: (0, 0))
    tile = pl.BlockSpec((BLK, D), lambda i, *_: (i, 0))
    half = (2 * WIN + 2) // 2
    return pl.pallas_call(
        attention_kernel,
        grid_spec=pltpu.PrefetchScalarGridSpec(
            num_scalar_prefetch=3,
            grid=(rows // BLK,),
            in_specs=[tile, whole(k.shape), whole(v.shape), tile, whole(w.shape)],
            out_specs=tile,
            scratch_shapes=[
                pltpu.VMEM((half, GROUP * BLK, 2 * BLK), F32),
                pltpu.VMEM((GROUP * BLK, BLK), F32),
                pltpu.VMEM((GROUP * BLK, BLK), F32),
                pltpu.VMEM((GROUP * BLK, SLAB), F32),
            ],
        ),
        out_shape=jax.ShapeDtypeStruct((rows, D), BF16),
        compiler_params=pltpu.CompilerParams(vmem_limit_bytes=48 * 2**20),
        cost_estimate=pl.CostEstimate(
            flops=16 * 10**9, bytes_accessed=8 * 2**20, transcendentals=rows * HEADS * 13 * BLK
        ),
    )(lists, counts, mult, q, k, v, mixed, w)


def tap_products(table, gain, taps):
    held = taps.shape[0]
    devices = lax.axis_size("batch")
    me = lax.axis_index("batch")
    spans = [(-(-(b + 1) * held // D)) - b * held // D for b in range(devices)]
    span = min(KERNEL, max(spans))

    def first(b):
        return jnp.minimum(b * held // D, KERNEL - span)

    normed = norm_rows(table.astype(F32), gain)
    begin = me * held
    copies = -(-held // D) + 1
    columns = lax.dynamic_slice_in_dim(jnp.tile(normed, (1, copies)), begin % D, held, 1)
    tap = (begin + jnp.arange(held, dtype=jnp.int32)) // D - first(me)
    mask = tap[None, :] == jnp.arange(span, dtype=jnp.int32)[:, None]
    spread = jnp.where(mask[:, None, :], columns[None], jnp.zeros((), BF16)).reshape(span * VOCAB, held)
    part = dot(spread, taps)
    total = jnp.zeros((KERNEL * VOCAB, D), F32)
    for step in range(devices):
        if step == 0:
            piece = part
        else:
            piece = lax.ppermute(part, "batch", [(b, (b + step) % devices) for b in range(devices)])
        place = first((me - step) % devices) * VOCAB
        total += lax.dynamic_update_slice_in_dim(jnp.zeros_like(total), piece, place, 0)
    return total


def local(codes, table, gains, taps, qkv, mixing, divisors, permitted):
    rows = codes.shape[1]
    rims = -(-WIN * BLK // rows)
    blocks = rows // BLK
    first_block = lax.axis_index("seq") * blocks
    total_blocks = blocks * lax.axis_size("seq")

    offsets = jnp.arange(-WIN, WIN + 1, dtype=jnp.int32)
    index = jnp.arange(blocks, dtype=jnp.int32)[:, None]
    target = first_block + index + offsets[None, :]
    allowed = (target >= 0) & (target < total_blocks)
    allowed = allowed[None] & ((permitted == 1) | (offsets == 0)[None, None])
    counts = jnp.sum(allowed.astype(jnp.int32), axis=-1)
    order = jnp.arange(2 * WIN + 1)
    place = jnp.sum(
        (allowed[:, :, None, :] & (order[None, :] < order[:, None])[None, None]).astype(jnp.int32), axis=-1
    )
    slots = jnp.arange(2 * WIN + 2, dtype=jnp.int32)
    picked = allowed[:, :, None, :] & (place[:, :, None, :] == slots[None, None, :, None])
    window = index + offsets[None, :] + rims * blocks
    lists = jnp.sum(jnp.where(picked, window[None, :, None, :], 0), axis=-1)
    mult = divisors * LOG2E

    margin = (rims + 1) * rows
    every = jnp.pad(lax.all_gather(codes[0], "seq", axis=0, tiled=True), (margin, margin), constant_values=-1)
    wide = lax.dynamic_slice_in_dim(every, lax.axis_index("seq") * rows, 2 * margin + rows, 0)
    begin = rows - KERNEL // 2
    span = (2 * rims + 1) * rows
    codes9 = jnp.stack([wide[begin + j : begin + j + span] for j in range(KERNEL)] + [wide[:span]] * (16 - KERNEL))
    products = tap_products(table, gains[0, 0], taps[0])
    high = products.astype(BF16)
    low = (products - high.astype(F32)).astype(BF16)
    w0 = lax.all_gather(qkv[0], "batch", axis=1, tiled=True)
    k, v, q, mixed = dense0(codes9, high, low, table, gains[0, 1][None], w0, rims)
    out0 = lax.all_gather(mixing[0], "batch", axis=0, tiled=True)
    stream = attention(lists[0], counts[0], mult[0], q, k, v, mixed, out0)

    taps1 = lax.all_gather(taps[1], "batch", axis=0, tiled=True)
    w1 = lax.all_gather(qkv[1], "batch", axis=1, tiled=True)
    out1 = lax.all_gather(mixing[1], "batch", axis=0, tiled=True)
    half = KERNEL // 2
    normed = norm_rows(stream.astype(F32), gains[1, 0])
    below = shifted(normed[rows - half :], "seq", 1)
    above = shifted(normed[:half], "seq", -1)
    padded = jnp.concatenate([below, normed, above], axis=0)
    unfold = jnp.concatenate([padded[j : j + rows] for j in range(KERNEL)], axis=1)
    conv = dot(unfold, taps1)
    mixed = (stream.astype(F32) + jax.nn.silu(conv)).astype(BF16)
    inputs = norm_rows(mixed.astype(F32), gains[1, 1])
    k, v, q = project(extend(inputs, "seq", rims), w1, rims)
    return attention(lists[1], counts[1], mult[1], q, k, v, mixed, out1)[None]


def solution(mesh):
    in_specs = (
        P("batch", "seq"),
        P(),
        P(),
        P(None, "batch", None),
        P(None, None, "batch"),
        P(None, "batch", None),
        P(),
        P(None, "seq", None),
    )
    out_specs = P("batch", "seq", None)
    return jax.shard_map(local, mesh=mesh, in_specs=in_specs, out_specs=out_specs, check_vma=False)
```

```python
import jax
import jax.numpy as jnp
from jax import lax
from jax.experimental import pallas as pl
from jax.experimental.pallas import tpu as pltpu
from jax.sharding import PartitionSpec as P

HEADS = 8
HEAD = 64
KERNEL = 9
VOCAB = 16
LAYERS = 2
BLK = 128
WIN = 12
D = 512
TILE = 512
GROUP = 4
SLAB = GROUP * HEAD
LOG2E = 1.4426950408889634
NARROW = 88.0
F32 = jnp.float32
BF16 = jnp.bfloat16


def exchange_kernel(reach, x_ref, out_ref, send_sem, recv_sem, local_sem):
    me = lax.axis_index("seq")
    devices = lax.axis_size("seq")
    steps = [sign * d for d in range(reach, 0, -1) for sign in (1, -1)]

    def present(other):
        return jnp.logical_and(other >= 0, other < devices)

    def copy(n, step):
        return pltpu.make_async_remote_copy(
            src_ref=x_ref,
            dst_ref=out_ref.at[reach - step],
            send_sem=send_sem.at[n],
            recv_sem=recv_sem.at[n],
            device_id={"seq": me + step},
            device_id_type=pl.DeviceIdType.MESH,
        )

    barrier = pltpu.get_barrier_semaphore()
    for step in steps:

        @pl.when(present(me + step))
        def _(step=step):
            pl.semaphore_signal(
                barrier, inc=1, device_id={"seq": me + step}, device_id_type=pl.DeviceIdType.MESH
            )

    pl.semaphore_wait(barrier, jnp.minimum(me, reach) + jnp.minimum(devices - 1 - me, reach))
    for n, step in enumerate(steps):

        @pl.when(present(me + step))
        def _(n=n, step=step):
            copy(n, step).start()

    own = pltpu.make_async_copy(x_ref, out_ref.at[reach], local_sem)
    own.start()
    for step in steps:

        @pl.when(jnp.logical_not(present(me - step)))
        def _(step=step):
            out_ref[reach - step] = jnp.zeros(x_ref.shape, x_ref.dtype)

    own.wait()
    for n, step in enumerate(steps):

        @pl.when(present(me + step))
        def _(n=n, step=step):
            copy(n, step).wait_send()

        @pl.when(present(me - step))
        def _(n=n, step=step):
            copy(n, step).wait_recv()


def exchange(x, reach, identity):
    return pl.pallas_call(
        lambda *refs: exchange_kernel(reach, *refs),
        in_specs=[pl.BlockSpec(memory_space=pltpu.VMEM)],
        out_specs=pl.BlockSpec(memory_space=pltpu.VMEM),
        out_shape=jax.ShapeDtypeStruct((2 * reach + 1,) + x.shape, x.dtype),
        scratch_shapes=[
            pltpu.SemaphoreType.DMA((2 * reach,)),
            pltpu.SemaphoreType.DMA((2 * reach,)),
            pltpu.SemaphoreType.DMA,
        ],
        compiler_params=pltpu.CompilerParams(
            collective_id=identity, has_side_effects=True, vmem_limit_bytes=24 * 2**20
        ),
    )(x)


def gather_ring(block, dim):
    devices = lax.axis_size("batch")
    me = lax.axis_index("batch")
    width = block.shape[dim]
    shape = list(block.shape)
    shape[dim] = devices * width
    total = jnp.zeros(shape, block.dtype)
    for step in range(devices):
        piece = block
        if step:
            piece = lax.ppermute(block, "batch", [(b, (b + step) % devices) for b in range(devices)])
        total = lax.dynamic_update_slice_in_dim(total, piece, (me - step) % devices * width, dim)
    return total


def dot(a, b):
    return jnp.dot(a, b, preferred_element_type=F32)


def norm_rows(values, gain):
    scaled = values * lax.rsqrt(jnp.mean(values * values, axis=-1, keepdims=True) + 1e-06)
    return (scaled * gain).astype(BF16)


def unit_heads(p):
    a = lax.broadcasted_iota(jnp.int32, (SLAB, SLAB), 0) // HEAD
    b = lax.broadcasted_iota(jnp.int32, (SLAB, SLAB), 1) // HEAD
    ones = (a == b).astype(F32).astype(BF16)
    parts = []
    for g in range(D // SLAB):
        piece = p[:, g * SLAB : (g + 1) * SLAB]
        square = piece * piece
        high = square.astype(BF16)
        low = (square - high.astype(F32)).astype(BF16)
        total = dot(high, ones) + dot(low, ones)
        scale = lax.rsqrt(total * (1.0 / HEAD) + 1e-06) * (1.0 / HEAD**0.5)
        parts.append((piece * scale).astype(BF16))
    return jnp.concatenate(parts, axis=1)


def dense0_kernel(own, codes_ref, high_ref, low_ref, table_ref, gain_ref, w_ref, k_ref, v_ref, q_ref, mixed_ref):
    vocab = lax.broadcasted_iota(jnp.int32, (VOCAB, TILE), 0)
    hot = [
        (codes_ref[j : j + 1, :] == vocab).astype(F32).astype(BF16) for j in range(KERNEL)
    ]
    dims = (((0,), (0,)), ((), ()))
    stream = lax.dot_general(hot[KERNEL // 2], table_ref[...], dims, preferred_element_type=F32)
    every = jnp.concatenate(hot, axis=0)
    conv = lax.dot_general(every, high_ref[...], dims, preferred_element_type=F32)
    conv += lax.dot_general(every, low_ref[...], dims, preferred_element_type=F32)
    mixed = (stream + conv / (1.0 + jnp.exp(-conv))).astype(BF16)
    inputs = norm_rows(mixed.astype(F32), gain_ref[...])
    k_ref[...] = unit_heads(dot(inputs, w_ref[:, D : 2 * D]))
    v_ref[...] = dot(inputs, w_ref[:, 2 * D :]).astype(BF16)

    @pl.when(pl.program_id(0) == own)
    def _():
        q_ref[...] = unit_heads(dot(inputs, w_ref[:, :D]))
        mixed_ref[...] = mixed


def dense0(codes9, high, low, table, gain, w, own):
    rows = codes9.shape[1]
    whole = lambda shape: pl.BlockSpec(shape, lambda i: (0, 0))
    tile = pl.BlockSpec((TILE, D), lambda i: (i, 0))
    return pl.pallas_call(
        lambda *refs: dense0_kernel(own, *refs),
        grid=(rows // TILE,),
        in_specs=[
            pl.BlockSpec((codes9.shape[0], TILE), lambda i: (0, i)),
            whole(high.shape),
            whole(low.shape),
            whole(table.shape),
            whole(gain.shape),
            whole(w.shape),
        ],
        out_specs=[tile, tile, whole((TILE, D)), whole((TILE, D))],
        out_shape=[jax.ShapeDtypeStruct((rows, D), BF16)] * 2
        + [jax.ShapeDtypeStruct((TILE, D), BF16)] * 2,
        compiler_params=pltpu.CompilerParams(vmem_limit_bytes=40 * 2**20),
        cost_estimate=pl.CostEstimate(
            flops=2 * rows * D * (3 * D), bytes_accessed=4 * rows * D + 2**21, transcendentals=rows * D
        ),
    )(codes9, high, low, table, gain, w)


def project_kernel(own, x_ref, w_ref, k_ref, v_ref, q_ref):
    inputs = x_ref[...]
    k_ref[...] = unit_heads(dot(inputs, w_ref[:, D : 2 * D]))
    v_ref[...] = dot(inputs, w_ref[:, 2 * D :]).astype(BF16)

    @pl.when(pl.program_id(0) == own)
    def _():
        q_ref[...] = unit_heads(dot(inputs, w_ref[:, :D]))


def project(x, w, own):
    rows = x.shape[0]
    whole = lambda shape: pl.BlockSpec(shape, lambda i: (0, 0))
    tile = pl.BlockSpec((TILE, D), lambda i: (i, 0))
    return pl.pallas_call(
        lambda *refs: project_kernel(own, *refs),
        grid=(rows // TILE,),
        in_specs=[tile, whole(w.shape)],
        out_specs=[tile, tile, whole((TILE, D))],
        out_shape=[jax.ShapeDtypeStruct((rows, D), BF16)] * 2
        + [jax.ShapeDtypeStruct((TILE, D), BF16)],
        compiler_params=pltpu.CompilerParams(vmem_limit_bytes=40 * 2**20),
        cost_estimate=pl.CostEstimate(
            flops=2 * rows * D * (2 * D), bytes_accessed=6 * rows * D + 2**21, transcendentals=rows * D
        ),
    )(x, w)


def attention_kernel(
    list_ref, count_ref, mult_ref, q_ref, k_ref, v_ref, mixed_ref, w_ref, out_ref, s_ref, m_ref, l_ref, acc_ref
):
    i = pl.program_id(0)
    count = count_ref[i]
    pairs = (count + 1) // 2
    lane = lax.broadcasted_iota(jnp.int32, (BLK, SLAB), 1) // HEAD
    joined = []

    def chunk(ref, p, g):
        first = pl.multiple_of(list_ref[i, 2 * p] * BLK, BLK)
        second = pl.multiple_of(list_ref[i, 2 * p + 1] * BLK, BLK)
        lanes = slice(g * SLAB, (g + 1) * SLAB)
        return jnp.concatenate([ref[pl.ds(first, BLK), lanes], ref[pl.ds(second, BLK), lanes]], axis=0)

    def gathered(ref, base, blocks, g):
        lanes = slice(g * SLAB, (g + 1) * SLAB)
        starts = [pl.multiple_of(list_ref[i, base + n] * BLK, BLK) for n in range(blocks)]
        return jnp.concatenate([ref[pl.ds(start, BLK), lanes] for start in starts], axis=0)

    for g in range(HEADS // GROUP):
        q = q_ref[:, g * SLAB : (g + 1) * SLAB]
        stacked = jnp.concatenate(
            [jnp.where(lane == h, q, jnp.zeros_like(q)) for h in range(GROUP)], axis=0
        )
        l_ref[...] = jnp.zeros_like(l_ref)
        acc_ref[...] = jnp.zeros_like(acc_ref)
        mults = [mult_ref[g * GROUP + h] for h in range(GROUP)]
        narrow = jnp.maximum(jnp.maximum(mults[0], mults[1]), jnp.maximum(mults[2], mults[3])) <= NARROW

        @pl.when(narrow)
        def _(g=g, stacked=stacked, mults=mults):
            def step(base, blocks, masked):
                keys, values = gathered(k_ref, base, blocks, g), gathered(v_ref, base, blocks, g)
                s = lax.dot_general(stacked, keys, (((1,), (1,)), ((), ())), preferred_element_type=F32)
                probs = []
                for h in range(GROUP):
                    rows = slice(h * BLK, (h + 1) * BLK)
                    scaled = s[rows] * mults[h]
                    if masked:
                        bias = jnp.where(base + 1 < count, 0.0, -1e30).astype(F32)
                        scaled = jnp.concatenate([scaled[:, :BLK], scaled[:, BLK:] + bias], axis=1)
                    expo = jnp.exp2(scaled)
                    part = expo[:, :BLK]
                    for n in range(1, blocks):
                        part += expo[:, n * BLK : (n + 1) * BLK]
                    l_ref[rows, :] += part
                    probs.append(expo.astype(BF16))
                acc_ref[...] += dot(jnp.concatenate(probs, axis=0), values)

            quads = count // 4
            lax.fori_loop(0, quads, lambda p, c: (step(4 * p, 4, False), c)[1], 0)
            rest = (count - 4 * quads + 1) // 2
            lax.fori_loop(0, rest, lambda p, c: (step(4 * quads + 2 * p, 2, True), c)[1], 0)

        @pl.when(jnp.logical_not(narrow))
        def _(g=g, stacked=stacked):
            m_ref[...] = jnp.full_like(m_ref, -1e30)

            def score(p, carry):
                s = lax.dot_general(
                    stacked, chunk(k_ref, p, g), (((1,), (1,)), ((), ())), preferred_element_type=F32
                )
                bias = jnp.where(2 * p + 1 < count, 0.0, -1e30).astype(F32)
                left, right = s[:, :BLK], s[:, BLK:] + bias
                s_ref[p, :, :BLK] = left
                s_ref[p, :, BLK:] = right
                m_ref[...] = jnp.maximum(m_ref[...], jnp.maximum(left, right))
                return carry

            lax.fori_loop(0, pairs, score, 0)
            for h in range(GROUP):
                rows = slice(h * BLK, (h + 1) * BLK)
                peak = jnp.max(m_ref[rows, :], axis=1, keepdims=True) * mult_ref[g * GROUP + h]
                m_ref[rows, :] = jnp.broadcast_to(peak, (BLK, BLK))

            def weigh(p, carry):
                probs = []
                for h in range(GROUP):
                    rows = slice(h * BLK, (h + 1) * BLK)
                    mult = mult_ref[g * GROUP + h]
                    peak = m_ref[rows, :]
                    left = jnp.exp2(s_ref[p, rows, :BLK] * mult - peak)
                    right = jnp.exp2(s_ref[p, rows, BLK:] * mult - peak)
                    l_ref[rows, :] += left + right
                    probs.append(jnp.concatenate([left.astype(BF16), right.astype(BF16)], axis=1))
                acc_ref[...] += dot(jnp.concatenate(probs, axis=0), chunk(v_ref, p, g))
                return carry

            lax.fori_loop(0, pairs, weigh, 0)
        result = jnp.zeros((BLK, SLAB), F32)
        for h in range(GROUP):
            rows = slice(h * BLK, (h + 1) * BLK)
            total = jnp.sum(l_ref[rows, :], axis=1, keepdims=True)
            result = jnp.where(lane == h, acc_ref[rows, :] * (1.0 / total), result)
        joined.append(result.astype(BF16))
    update = dot(jnp.concatenate(joined, axis=1), w_ref[...])
    out_ref[...] = (mixed_ref[...].astype(F32) + update).astype(BF16)


def attention(lists, counts, mult, q, k, v, mixed, w):
    rows = q.shape[0]
    whole = lambda shape: pl.BlockSpec(shape, lambda i, *_: (0, 0))
    tile = pl.BlockSpec((BLK, D), lambda i, *_: (i, 0))
    half = (2 * WIN + 2) // 2
    return pl.pallas_call(
        attention_kernel,
        grid_spec=pltpu.PrefetchScalarGridSpec(
            num_scalar_prefetch=3,
            grid=(rows // BLK,),
            in_specs=[tile, whole(k.shape), whole(v.shape), tile, whole(w.shape)],
            out_specs=tile,
            scratch_shapes=[
                pltpu.VMEM((half, GROUP * BLK, 2 * BLK), F32),
                pltpu.VMEM((GROUP * BLK, BLK), F32),
                pltpu.VMEM((GROUP * BLK, BLK), F32),
                pltpu.VMEM((GROUP * BLK, SLAB), F32),
            ],
        ),
        out_shape=jax.ShapeDtypeStruct((rows, D), BF16),
        compiler_params=pltpu.CompilerParams(vmem_limit_bytes=48 * 2**20),
        cost_estimate=pl.CostEstimate(
            flops=16 * 10**9, bytes_accessed=8 * 2**20, transcendentals=rows * HEADS * 13 * BLK
        ),
    )(lists, counts, mult, q, k, v, mixed, w)


def tap_products(table, gain, taps):
    held = taps.shape[0]
    devices = lax.axis_size("batch")
    me = lax.axis_index("batch")
    spans = [(-(-(b + 1) * held // D)) - b * held // D for b in range(devices)]
    span = min(KERNEL, max(spans))

    def first(b):
        return jnp.minimum(b * held // D, KERNEL - span)

    normed = norm_rows(table.astype(F32), gain)
    begin = me * held
    copies = -(-held // D) + 1
    columns = lax.dynamic_slice_in_dim(jnp.tile(normed, (1, copies)), begin % D, held, 1)
    tap = (begin + jnp.arange(held, dtype=jnp.int32)) // D - first(me)
    mask = tap[None, :] == jnp.arange(span, dtype=jnp.int32)[:, None]
    spread = jnp.where(mask[:, None, :], columns[None], jnp.zeros((), BF16)).reshape(span * VOCAB, held)
    part = dot(spread, taps)
    total = jnp.zeros((KERNEL * VOCAB, D), F32)
    for step in range(devices):
        if step == 0:
            piece = part
        else:
            piece = lax.ppermute(part, "batch", [(b, (b + step) % devices) for b in range(devices)])
        place = first((me - step) % devices) * VOCAB
        total += lax.dynamic_update_slice_in_dim(jnp.zeros_like(total), piece, place, 0)
    return total


def local(codes, table, gains, taps, qkv, mixing, divisors, permitted):
    rows = codes.shape[1]
    rims = -(-WIN * BLK // rows)
    blocks = rows // BLK
    first_block = lax.axis_index("seq") * blocks
    total_blocks = blocks * lax.axis_size("seq")

    offsets = jnp.arange(-WIN, WIN + 1, dtype=jnp.int32)
    index = jnp.arange(blocks, dtype=jnp.int32)[:, None]
    target = first_block + index + offsets[None, :]
    allowed = (target >= 0) & (target < total_blocks)
    allowed = allowed[None] & ((permitted == 1) | (offsets == 0)[None, None])
    counts = jnp.sum(allowed.astype(jnp.int32), axis=-1)
    order = jnp.arange(2 * WIN + 1)
    place = jnp.sum(
        (allowed[:, :, None, :] & (order[None, :] < order[:, None])[None, None]).astype(jnp.int32), axis=-1
    )
    slots = jnp.arange(2 * WIN + 2, dtype=jnp.int32)
    picked = allowed[:, :, None, :] & (place[:, :, None, :] == slots[None, None, :, None])
    window = index + offsets[None, :] + rims * blocks
    lists = jnp.sum(jnp.where(picked, window[None, :, None, :], 0), axis=-1)
    mult = divisors * LOG2E

    wide = exchange(codes[0].reshape(-1, BLK) + 1, rims + 1, 0).reshape(-1) - 1
    begin = rows - KERNEL // 2
    span = (2 * rims + 1) * rows
    codes9 = jnp.stack([wide[begin + j : begin + j + span] for j in range(KERNEL)] + [wide[:span]] * (16 - KERNEL))
    products = tap_products(table, gains[0, 0], taps[0])
    high = products.astype(BF16)
    low = (products - high.astype(F32)).astype(BF16)
    outs = gather_ring(mixing, 1)
    w0 = lax.all_gather(qkv[0], "batch", axis=1, tiled=True)
    k, v, q, mixed = dense0(codes9, high, low, table, gains[0, 1][None], w0, rims)
    stream = attention(lists[0], counts[0], mult[0], q, k, v, mixed, outs[0])

    taps1 = lax.all_gather(taps[1], "batch", axis=0, tiled=True)
    w1 = lax.all_gather(qkv[1], "batch", axis=1, tiled=True)
    half = KERNEL // 2
    normed = norm_rows(stream.astype(F32), gains[1, 0])
    edges = exchange(jnp.concatenate([normed[:8], normed[rows - 8 :]], axis=0), 1, 1)
    padded = jnp.concatenate([edges[0, 16 - half :], normed, edges[2, :half]], axis=0)
    unfold = jnp.concatenate([padded[j : j + rows] for j in range(KERNEL)], axis=1)
    conv = dot(unfold, taps1)
    mixed = (stream.astype(F32) + jax.nn.silu(conv)).astype(BF16)
    inputs = norm_rows(mixed.astype(F32), gains[1, 1])
    k, v, q = project(exchange(inputs, rims, 2).reshape(-1, D), w1, rims)
    return attention(lists[1], counts[1], mult[1], q, k, v, mixed, outs[1])[None]


def solution(mesh):
    in_specs = (
        P("batch", "seq"),
        P(),
        P(),
        P(None, "batch", None),
        P(None, None, "batch"),
        P(None, "batch", None),
        P(),
        P(None, "seq", None),
    )
    out_specs = P("batch", "seq", None)
    return jax.shard_map(local, mesh=mesh, in_specs=in_specs, out_specs=out_specs, check_vma=False)
```

```python
import jax
import jax.numpy as jnp
from jax import lax
from jax.experimental import pallas as pl
from jax.experimental.pallas import tpu as pltpu
from jax.sharding import PartitionSpec as P

HEADS = 8
HEAD = 64
KERNEL = 9
VOCAB = 16
LAYERS = 2
BLK = 128
WIN = 12
D = 512
TILE = 512
GROUP = 4
SLAB = GROUP * HEAD
LOG2E = 1.4426950408889634
NARROW = 88.0
F32 = jnp.float32
BF16 = jnp.bfloat16


def exchange_kernel(reach, x_ref, out_ref, send_sem, recv_sem, local_sem):
    me = lax.axis_index("seq")
    devices = lax.axis_size("seq")
    steps = [sign * d for d in range(reach, 0, -1) for sign in (1, -1)]

    def present(other):
        return jnp.logical_and(other >= 0, other < devices)

    def copy(n, step):
        return pltpu.make_async_remote_copy(
            src_ref=x_ref,
            dst_ref=out_ref.at[reach - step],
            send_sem=send_sem.at[n],
            recv_sem=recv_sem.at[n],
            device_id={"seq": me + step},
            device_id_type=pl.DeviceIdType.MESH,
        )

    barrier = pltpu.get_barrier_semaphore()
    for step in steps:

        @pl.when(present(me + step))
        def _(step=step):
            pl.semaphore_signal(
                barrier, inc=1, device_id={"seq": me + step}, device_id_type=pl.DeviceIdType.MESH
            )

    pl.semaphore_wait(barrier, jnp.minimum(me, reach) + jnp.minimum(devices - 1 - me, reach))
    for n, step in enumerate(steps):

        @pl.when(present(me + step))
        def _(n=n, step=step):
            copy(n, step).start()

    own = pltpu.make_async_copy(x_ref, out_ref.at[reach], local_sem)
    own.start()
    for step in steps:

        @pl.when(jnp.logical_not(present(me - step)))
        def _(step=step):
            out_ref[reach - step] = jnp.zeros(x_ref.shape, x_ref.dtype)

    own.wait()
    for n, step in enumerate(steps):

        @pl.when(present(me + step))
        def _(n=n, step=step):
            copy(n, step).wait_send()

        @pl.when(present(me - step))
        def _(n=n, step=step):
            copy(n, step).wait_recv()


def exchange(x, reach, identity):
    return pl.pallas_call(
        lambda *refs: exchange_kernel(reach, *refs),
        in_specs=[pl.BlockSpec(memory_space=pltpu.VMEM)],
        out_specs=pl.BlockSpec(memory_space=pltpu.VMEM),
        out_shape=jax.ShapeDtypeStruct((2 * reach + 1,) + x.shape, x.dtype),
        scratch_shapes=[
            pltpu.SemaphoreType.DMA((2 * reach,)),
            pltpu.SemaphoreType.DMA((2 * reach,)),
            pltpu.SemaphoreType.DMA,
        ],
        compiler_params=pltpu.CompilerParams(
            collective_id=identity, has_side_effects=True, vmem_limit_bytes=24 * 2**20
        ),
    )(x)


def relay_kernel(x_ref, out_ref, send_sem, recv_sem, local_sem):
    me = lax.axis_index("seq")
    devices = lax.axis_size("seq")
    side = 1 - 2 * lax.rem(me, 2)
    mate = me + side

    def present(other):
        return jnp.logical_and(other >= 0, other < devices)

    def copy(n, source, slot, target):
        return pltpu.make_async_remote_copy(
            src_ref=source,
            dst_ref=out_ref.at[slot],
            send_sem=send_sem.at[n],
            recv_sem=recv_sem.at[n],
            device_id={"seq": target},
            device_id_type=pl.DeviceIdType.MESH,
        )

    far = me - 3 * side
    direct = [
        (3, x_ref, 3 + 3 * side, far, 3 - 3 * side, present(far), present(far)),
        (1, x_ref, 1, me + 2, 1, present(me + 2), present(me - 2)),
        (2, x_ref, 5, me - 2, 5, present(me - 2), present(me + 2)),
    ]
    passed = [
        (4, out_ref.at[1], 1 - side, mate, 1 + side, present(me - 2), present(mate - 2)),
        (5, out_ref.at[5], 5 - side, mate, 5 + side, present(me + 2), present(mate + 2)),
    ]
    barrier = pltpu.get_barrier_semaphore()

    def greet(target):
        pl.semaphore_signal(barrier, inc=1, device_id={"seq": target}, device_id_type=pl.DeviceIdType.MESH)

    greet(mate)
    for entry in direct:

        @pl.when(entry[5])
        def _(entry=entry):
            greet(entry[3])

    pl.semaphore_wait(barrier, 1 + sum(jnp.where(entry[5], 1, 0) for entry in direct))
    for n, source, there, target, here, sends, receives in direct:

        @pl.when(sends)
        def _(n=n, source=source, there=there, target=target):
            copy(n, source, there, target).start()

    first = copy(0, x_ref, 3 - side, mate)
    first.start()
    own = pltpu.make_async_copy(x_ref, out_ref.at[3], local_sem)
    own.start()
    for step in (-3, -2, -1, 1, 2, 3):

        @pl.when(jnp.logical_not(present(me - step)))
        def _(step=step):
            out_ref[3 - step] = jnp.zeros(x_ref.shape, x_ref.dtype)

    own.wait()
    first.wait_send()
    copy(0, x_ref, 3 + side, mate).wait_recv()
    for entry, hand in zip(direct[1:], passed):

        @pl.when(entry[6])
        def _(entry=entry, hand=hand):
            copy(entry[0], x_ref, entry[4], entry[3]).wait_recv()
            copy(hand[0], hand[1], hand[2], mate).start()

    for n, source, there, target, here, sends, receives in direct + passed:

        @pl.when(sends)
        def _(n=n, source=source, there=there, target=target):
            copy(n, source, there, target).wait_send()

    for n, source, there, target, here, sends, receives in direct[:1] + passed:

        @pl.when(receives)
        def _(n=n, here=here, target=target):
            copy(n, x_ref, here, target).wait_recv()


def relay(x, identity):
    return pl.pallas_call(
        relay_kernel,
        in_specs=[pl.BlockSpec(memory_space=pltpu.VMEM)],
        out_specs=pl.BlockSpec(memory_space=pltpu.VMEM),
        out_shape=jax.ShapeDtypeStruct((7,) + x.shape, x.dtype),
        scratch_shapes=[
            pltpu.SemaphoreType.DMA((6,)),
            pltpu.SemaphoreType.DMA((6,)),
            pltpu.SemaphoreType.DMA,
        ],
        compiler_params=pltpu.CompilerParams(
            collective_id=identity, has_side_effects=True, vmem_limit_bytes=24 * 2**20
        ),
    )(x)


def shared_gather(block):
    core = lax.axis_index("seq") % 2
    half = block.shape[0] // 2
    mine = lax.dynamic_slice_in_dim(block, core * half, half, 0)
    mine = lax.all_gather(mine, "batch", axis=0, tiled=False)
    other = lax.ppermute(mine, "seq", [(i, i ^ 1) for i in range(lax.axis_size("seq"))])
    even = core == 0
    return jnp.concatenate([jnp.where(even, mine, other), jnp.where(even, other, mine)], axis=1)


def gather_ring(block, dim):
    devices = lax.axis_size("batch")
    me = lax.axis_index("batch")
    width = block.shape[dim]
    shape = list(block.shape)
    shape[dim] = devices * width
    total = jnp.zeros(shape, block.dtype)
    for step in range(devices):
        piece = block
        if step:
            piece = lax.ppermute(block, "batch", [(b, (b + step) % devices) for b in range(devices)])
        total = lax.dynamic_update_slice_in_dim(total, piece, (me - step) % devices * width, dim)
    return total


def dot(a, b):
    return jnp.dot(a, b, preferred_element_type=F32)


def norm_rows(values, gain):
    scaled = values * lax.rsqrt(jnp.mean(values * values, axis=-1, keepdims=True) + 1e-06)
    return (scaled * gain).astype(BF16)


def unit_heads(p):
    a = lax.broadcasted_iota(jnp.int32, (SLAB, SLAB), 0) // HEAD
    b = lax.broadcasted_iota(jnp.int32, (SLAB, SLAB), 1) // HEAD
    ones = (a == b).astype(F32).astype(BF16)
    parts = []
    for g in range(D // SLAB):
        piece = p[:, g * SLAB : (g + 1) * SLAB]
        square = piece * piece
        high = square.astype(BF16)
        low = (square - high.astype(F32)).astype(BF16)
        total = dot(high, ones) + dot(low, ones)
        scale = lax.rsqrt(total * (1.0 / HEAD) + 1e-06) * (1.0 / HEAD**0.5)
        parts.append((piece * scale).astype(BF16))
    return jnp.concatenate(parts, axis=1)


def dense0_kernel(own, codes_ref, high_ref, low_ref, table_ref, gain_ref, w_ref, k_ref, v_ref, q_ref, mixed_ref):
    vocab = lax.broadcasted_iota(jnp.int32, (VOCAB, TILE), 0)
    hot = [
        (codes_ref[j : j + 1, :] == vocab).astype(F32).astype(BF16) for j in range(KERNEL)
    ]
    dims = (((0,), (0,)), ((), ()))
    stream = lax.dot_general(hot[KERNEL // 2], table_ref[...], dims, preferred_element_type=F32)
    every = jnp.concatenate(hot, axis=0)
    conv = lax.dot_general(every, high_ref[...], dims, preferred_element_type=F32)
    conv += lax.dot_general(every, low_ref[...], dims, preferred_element_type=F32)
    mixed = (stream + conv / (1.0 + jnp.exp(-conv))).astype(BF16)
    inputs = norm_rows(mixed.astype(F32), gain_ref[...])
    k_ref[...] = unit_heads(dot(inputs, w_ref[:, D : 2 * D]))
    v_ref[...] = dot(inputs, w_ref[:, 2 * D :]).astype(BF16)

    @pl.when(pl.program_id(0) == own)
    def _():
        q_ref[...] = unit_heads(dot(inputs, w_ref[:, :D]))
        mixed_ref[...] = mixed


def dense0(codes9, high, low, table, gain, w, own):
    rows = codes9.shape[1]
    whole = lambda shape: pl.BlockSpec(shape, lambda i: (0, 0))
    tile = pl.BlockSpec((TILE, D), lambda i: (i, 0))
    return pl.pallas_call(
        lambda *refs: dense0_kernel(own, *refs),
        grid=(rows // TILE,),
        in_specs=[
            pl.BlockSpec((codes9.shape[0], TILE), lambda i: (0, i)),
            whole(high.shape),
            whole(low.shape),
            whole(table.shape),
            whole(gain.shape),
            whole(w.shape),
        ],
        out_specs=[tile, tile, whole((TILE, D)), whole((TILE, D))],
        out_shape=[jax.ShapeDtypeStruct((rows, D), BF16)] * 2
        + [jax.ShapeDtypeStruct((TILE, D), BF16)] * 2,
        compiler_params=pltpu.CompilerParams(vmem_limit_bytes=40 * 2**20),
        cost_estimate=pl.CostEstimate(
            flops=2 * rows * D * (3 * D), bytes_accessed=4 * rows * D + 2**21, transcendentals=rows * D
        ),
    )(codes9, high, low, table, gain, w)


def project_kernel(own, x_ref, w_ref, k_ref, v_ref, q_ref):
    inputs = x_ref[...]
    k_ref[...] = unit_heads(dot(inputs, w_ref[:, D : 2 * D]))
    v_ref[...] = dot(inputs, w_ref[:, 2 * D :]).astype(BF16)

    @pl.when(pl.program_id(0) == own)
    def _():
        q_ref[...] = unit_heads(dot(inputs, w_ref[:, :D]))


def project(x, w, own):
    rows = x.shape[0]
    whole = lambda shape: pl.BlockSpec(shape, lambda i: (0, 0))
    tile = pl.BlockSpec((TILE, D), lambda i: (i, 0))
    return pl.pallas_call(
        lambda *refs: project_kernel(own, *refs),
        grid=(rows // TILE,),
        in_specs=[tile, whole(w.shape)],
        out_specs=[tile, tile, whole((TILE, D))],
        out_shape=[jax.ShapeDtypeStruct((rows, D), BF16)] * 2
        + [jax.ShapeDtypeStruct((TILE, D), BF16)],
        compiler_params=pltpu.CompilerParams(vmem_limit_bytes=40 * 2**20),
        cost_estimate=pl.CostEstimate(
            flops=2 * rows * D * (2 * D), bytes_accessed=6 * rows * D + 2**21, transcendentals=rows * D
        ),
    )(x, w)


def attention_kernel(
    list_ref, count_ref, mult_ref, q_ref, k_ref, v_ref, mixed_ref, w_ref, out_ref, s_ref, m_ref, l_ref, acc_ref
):
    i = pl.program_id(0)
    count = count_ref[i]
    pairs = (count + 1) // 2
    lane = lax.broadcasted_iota(jnp.int32, (BLK, SLAB), 1) // HEAD
    joined = []

    def chunk(ref, p, g):
        first = pl.multiple_of(list_ref[i, 2 * p] * BLK, BLK)
        second = pl.multiple_of(list_ref[i, 2 * p + 1] * BLK, BLK)
        lanes = slice(g * SLAB, (g + 1) * SLAB)
        return jnp.concatenate([ref[pl.ds(first, BLK), lanes], ref[pl.ds(second, BLK), lanes]], axis=0)

    def gathered(ref, base, blocks, g):
        lanes = slice(g * SLAB, (g + 1) * SLAB)
        starts = [pl.multiple_of(list_ref[i, base + n] * BLK, BLK) for n in range(blocks)]
        return jnp.concatenate([ref[pl.ds(start, BLK), lanes] for start in starts], axis=0)

    for g in range(HEADS // GROUP):
        q = q_ref[:, g * SLAB : (g + 1) * SLAB]
        stacked = jnp.concatenate(
            [jnp.where(lane == h, q, jnp.zeros_like(q)) for h in range(GROUP)], axis=0
        )
        l_ref[...] = jnp.zeros_like(l_ref)
        acc_ref[...] = jnp.zeros_like(acc_ref)
        mults = [mult_ref[g * GROUP + h] for h in range(GROUP)]
        narrow = jnp.maximum(jnp.maximum(mults[0], mults[1]), jnp.maximum(mults[2], mults[3])) <= NARROW

        @pl.when(narrow)
        def _(g=g, stacked=stacked, mults=mults):
            def step(base, blocks, masked):
                keys, values = gathered(k_ref, base, blocks, g), gathered(v_ref, base, blocks, g)
                s = lax.dot_general(stacked, keys, (((1,), (1,)), ((), ())), preferred_element_type=F32)
                probs = []
                for h in range(GROUP):
                    rows = slice(h * BLK, (h + 1) * BLK)
                    scaled = s[rows] * mults[h]
                    if masked:
                        bias = jnp.where(base + 1 < count, 0.0, -1e30).astype(F32)
                        scaled = jnp.concatenate([scaled[:, :BLK], scaled[:, BLK:] + bias], axis=1)
                    expo = jnp.exp2(scaled)
                    part = expo[:, :BLK]
                    for n in range(1, blocks):
                        part += expo[:, n * BLK : (n + 1) * BLK]
                    l_ref[rows, :] += part
                    probs.append(expo.astype(BF16))
                acc_ref[...] += dot(jnp.concatenate(probs, axis=0), values)

            quads = count // 4
            lax.fori_loop(0, quads, lambda p, c: (step(4 * p, 4, False), c)[1], 0)
            rest = (count - 4 * quads + 1) // 2
            lax.fori_loop(0, rest, lambda p, c: (step(4 * quads + 2 * p, 2, True), c)[1], 0)

        @pl.when(jnp.logical_not(narrow))
        def _(g=g, stacked=stacked):
            m_ref[...] = jnp.full_like(m_ref, -1e30)

            def score(p, carry):
                s = lax.dot_general(
                    stacked, chunk(k_ref, p, g), (((1,), (1,)), ((), ())), preferred_element_type=F32
                )
                bias = jnp.where(2 * p + 1 < count, 0.0, -1e30).astype(F32)
                left, right = s[:, :BLK], s[:, BLK:] + bias
                s_ref[p, :, :BLK] = left
                s_ref[p, :, BLK:] = right
                m_ref[...] = jnp.maximum(m_ref[...], jnp.maximum(left, right))
                return carry

            lax.fori_loop(0, pairs, score, 0)
            for h in range(GROUP):
                rows = slice(h * BLK, (h + 1) * BLK)
                peak = jnp.max(m_ref[rows, :], axis=1, keepdims=True) * mult_ref[g * GROUP + h]
                m_ref[rows, :] = jnp.broadcast_to(peak, (BLK, BLK))

            def weigh(p, carry):
                probs = []
                for h in range(GROUP):
                    rows = slice(h * BLK, (h + 1) * BLK)
                    mult = mult_ref[g * GROUP + h]
                    peak = m_ref[rows, :]
                    left = jnp.exp2(s_ref[p, rows, :BLK] * mult - peak)
                    right = jnp.exp2(s_ref[p, rows, BLK:] * mult - peak)
                    l_ref[rows, :] += left + right
                    probs.append(jnp.concatenate([left.astype(BF16), right.astype(BF16)], axis=1))
                acc_ref[...] += dot(jnp.concatenate(probs, axis=0), chunk(v_ref, p, g))
                return carry

            lax.fori_loop(0, pairs, weigh, 0)
        result = jnp.zeros((BLK, SLAB), F32)
        for h in range(GROUP):
            rows = slice(h * BLK, (h + 1) * BLK)
            total = jnp.sum(l_ref[rows, :], axis=1, keepdims=True)
            result = jnp.where(lane == h, acc_ref[rows, :] * (1.0 / total), result)
        joined.append(result.astype(BF16))
    update = dot(jnp.concatenate(joined, axis=1), w_ref[...])
    out_ref[...] = (mixed_ref[...].astype(F32) + update).astype(BF16)


def attention(lists, counts, mult, q, k, v, mixed, w):
    rows = q.shape[0]
    whole = lambda shape: pl.BlockSpec(shape, lambda i, *_: (0, 0))
    tile = pl.BlockSpec((BLK, D), lambda i, *_: (i, 0))
    half = (2 * WIN + 2) // 2
    return pl.pallas_call(
        attention_kernel,
        grid_spec=pltpu.PrefetchScalarGridSpec(
            num_scalar_prefetch=3,
            grid=(rows // BLK,),
            in_specs=[tile, whole(k.shape), whole(v.shape), tile, whole(w.shape)],
            out_specs=tile,
            scratch_shapes=[
                pltpu.VMEM((half, GROUP * BLK, 2 * BLK), F32),
                pltpu.VMEM((GROUP * BLK, BLK), F32),
                pltpu.VMEM((GROUP * BLK, BLK), F32),
                pltpu.VMEM((GROUP * BLK, SLAB), F32),
            ],
        ),
        out_shape=jax.ShapeDtypeStruct((rows, D), BF16),
        compiler_params=pltpu.CompilerParams(vmem_limit_bytes=48 * 2**20),
        cost_estimate=pl.CostEstimate(
            flops=16 * 10**9, bytes_accessed=8 * 2**20, transcendentals=rows * HEADS * 13 * BLK
        ),
    )(lists, counts, mult, q, k, v, mixed, w)


def tap_products(table, gain, taps):
    held = taps.shape[0]
    devices = lax.axis_size("batch")
    me = lax.axis_index("batch")
    spans = [(-(-(b + 1) * held // D)) - b * held // D for b in range(devices)]
    span = min(KERNEL, max(spans))

    def first(b):
        return jnp.minimum(b * held // D, KERNEL - span)

    normed = norm_rows(table.astype(F32), gain)
    begin = me * held
    copies = -(-held // D) + 1
    columns = lax.dynamic_slice_in_dim(jnp.tile(normed, (1, copies)), begin % D, held, 1)
    tap = (begin + jnp.arange(held, dtype=jnp.int32)) // D - first(me)
    mask = tap[None, :] == jnp.arange(span, dtype=jnp.int32)[:, None]
    spread = jnp.where(mask[:, None, :], columns[None], jnp.zeros((), BF16)).reshape(span * VOCAB, held)
    part = dot(spread, taps)
    total = jnp.zeros((KERNEL * VOCAB, D), F32)
    for step in range(devices):
        if step == 0:
            piece = part
        else:
            piece = lax.ppermute(part, "batch", [(b, (b + step) % devices) for b in range(devices)])
        place = first((me - step) % devices) * VOCAB
        total += lax.dynamic_update_slice_in_dim(jnp.zeros_like(total), piece, place, 0)
    return total


def local(codes, table, gains, taps, qkv, mixing, divisors, permitted):
    rows = codes.shape[1]
    rims = -(-WIN * BLK // rows)
    blocks = rows // BLK
    first_block = lax.axis_index("seq") * blocks
    total_blocks = blocks * lax.axis_size("seq")

    offsets = jnp.arange(-WIN, WIN + 1, dtype=jnp.int32)
    index = jnp.arange(blocks, dtype=jnp.int32)[:, None]
    target = first_block + index + offsets[None, :]
    allowed = (target >= 0) & (target < total_blocks)
    allowed = allowed[None] & ((permitted == 1) | (offsets == 0)[None, None])
    counts = jnp.sum(allowed.astype(jnp.int32), axis=-1)
    order = jnp.arange(2 * WIN + 1)
    place = jnp.sum(
        (allowed[:, :, None, :] & (order[None, :] < order[:, None])[None, None]).astype(jnp.int32), axis=-1
    )
    slots = jnp.arange(2 * WIN + 2, dtype=jnp.int32)
    picked = allowed[:, :, None, :] & (place[:, :, None, :] == slots[None, None, :, None])
    window = index + offsets[None, :] + rims * blocks
    lists = jnp.sum(jnp.where(picked, window[None, :, None, :], 0), axis=-1)
    mult = divisors * LOG2E

    wide = exchange(codes[0].reshape(-1, BLK) + 1, rims + 1, 0).reshape(-1) - 1
    begin = rows - KERNEL // 2
    span = (2 * rims + 1) * rows
    codes9 = jnp.stack([wide[begin + j : begin + j + span] for j in range(KERNEL)] + [wide[:span]] * (16 - KERNEL))
    products = tap_products(table, gains[0, 0], taps[0])
    high = products.astype(BF16)
    low = (products - high.astype(F32)).astype(BF16)
    outs = gather_ring(mixing, 1)
    w0 = lax.all_gather(qkv[0], "batch", axis=1, tiled=True)
    k, v, q, mixed = dense0(codes9, high, low, table, gains[0, 1][None], w0, rims)
    stream = attention(lists[0], counts[0], mult[0], q, k, v, mixed, outs[0])

    taps1 = shared_gather(taps[1]).reshape(KERNEL * D, D)
    w1 = lax.all_gather(qkv[1], "batch", axis=1, tiled=True)
    half = KERNEL // 2
    normed = norm_rows(stream.astype(F32), gains[1, 0])
    edges = exchange(jnp.concatenate([normed[:8], normed[rows - 8 :]], axis=0), 1, 1)
    padded = jnp.concatenate([edges[0, 16 - half :], normed, edges[2, :half]], axis=0)
    unfold = jnp.concatenate([padded[j : j + rows] for j in range(KERNEL)], axis=1)
    conv = dot(unfold, taps1)
    mixed = (stream.astype(F32) + jax.nn.silu(conv)).astype(BF16)
    inputs = norm_rows(mixed.astype(F32), gains[1, 1])
    k, v, q = project((relay(inputs, 2) if rims == 3 else exchange(inputs, rims, 2)).reshape(-1, D), w1, rims)
    return attention(lists[1], counts[1], mult[1], q, k, v, mixed, outs[1])[None]


def solution(mesh):
    in_specs = (
        P("batch", "seq"),
        P(),
        P(),
        P(None, "batch", None),
        P(None, None, "batch"),
        P(None, "batch", None),
        P(),
        P(None, "seq", None),
    )
    out_specs = P("batch", "seq", None)
    return jax.shard_map(local, mesh=mesh, in_specs=in_specs, out_specs=out_specs, check_vma=False)
```

```python
import jax
import jax.numpy as jnp
from jax import lax
from jax.experimental import pallas as pl
from jax.experimental.pallas import tpu as pltpu
from jax.sharding import PartitionSpec as P

HEADS = 8
HEAD = 64
KERNEL = 9
VOCAB = 16
LAYERS = 2
BLK = 128
WIN = 12
D = 512
TILE = 512
GROUP = 4
SLAB = GROUP * HEAD
LOG2E = 1.4426950408889634
NARROW = 88.0
F32 = jnp.float32
BF16 = jnp.bfloat16


def exchange_kernel(reach, x_ref, out_ref, send_sem, recv_sem, local_sem):
    me = lax.axis_index("seq")
    devices = lax.axis_size("seq")
    steps = [sign * d for d in range(reach, 0, -1) for sign in (1, -1)]

    def present(other):
        return jnp.logical_and(other >= 0, other < devices)

    def copy(n, step):
        return pltpu.make_async_remote_copy(
            src_ref=x_ref,
            dst_ref=out_ref.at[reach - step],
            send_sem=send_sem.at[n],
            recv_sem=recv_sem.at[n],
            device_id={"seq": me + step},
            device_id_type=pl.DeviceIdType.MESH,
        )

    barrier = pltpu.get_barrier_semaphore()
    for step in steps:

        @pl.when(present(me + step))
        def _(step=step):
            pl.semaphore_signal(
                barrier, inc=1, device_id={"seq": me + step}, device_id_type=pl.DeviceIdType.MESH
            )

    pl.semaphore_wait(barrier, jnp.minimum(me, reach) + jnp.minimum(devices - 1 - me, reach))
    for n, step in enumerate(steps):

        @pl.when(present(me + step))
        def _(n=n, step=step):
            copy(n, step).start()

    own = pltpu.make_async_copy(x_ref, out_ref.at[reach], local_sem)
    own.start()
    for step in steps:

        @pl.when(jnp.logical_not(present(me - step)))
        def _(step=step):
            out_ref[reach - step] = jnp.zeros(x_ref.shape, x_ref.dtype)

    own.wait()
    for n, step in enumerate(steps):

        @pl.when(present(me + step))
        def _(n=n, step=step):
            copy(n, step).wait_send()

        @pl.when(present(me - step))
        def _(n=n, step=step):
            copy(n, step).wait_recv()


def exchange(x, reach, identity):
    return pl.pallas_call(
        lambda *refs: exchange_kernel(reach, *refs),
        in_specs=[pl.BlockSpec(memory_space=pltpu.VMEM)],
        out_specs=pl.BlockSpec(memory_space=pltpu.VMEM),
        out_shape=jax.ShapeDtypeStruct((2 * reach + 1,) + x.shape, x.dtype),
        scratch_shapes=[
            pltpu.SemaphoreType.DMA((2 * reach,)),
            pltpu.SemaphoreType.DMA((2 * reach,)),
            pltpu.SemaphoreType.DMA,
        ],
        compiler_params=pltpu.CompilerParams(
            collective_id=identity, has_side_effects=True, vmem_limit_bytes=24 * 2**20
        ),
    )(x)


def relay_kernel(x_ref, out_ref, send_sem, recv_sem, local_sem):
    me = lax.axis_index("seq")
    devices = lax.axis_size("seq")
    side = 1 - 2 * lax.rem(me, 2)
    mate = me + side

    def present(other):
        return jnp.logical_and(other >= 0, other < devices)

    def copy(n, source, slot, target):
        return pltpu.make_async_remote_copy(
            src_ref=source,
            dst_ref=out_ref.at[slot],
            send_sem=send_sem.at[n],
            recv_sem=recv_sem.at[n],
            device_id={"seq": target},
            device_id_type=pl.DeviceIdType.MESH,
        )

    far = me - 3 * side
    direct = [
        (3, x_ref, 3 + 3 * side, far, 3 - 3 * side, present(far), present(far)),
        (1, x_ref, 1, me + 2, 1, present(me + 2), present(me - 2)),
        (2, x_ref, 5, me - 2, 5, present(me - 2), present(me + 2)),
    ]
    passed = [
        (4, out_ref.at[1], 1 - side, mate, 1 + side, present(me - 2), present(mate - 2)),
        (5, out_ref.at[5], 5 - side, mate, 5 + side, present(me + 2), present(mate + 2)),
    ]
    barrier = pltpu.get_barrier_semaphore()

    def greet(target):
        pl.semaphore_signal(barrier, inc=1, device_id={"seq": target}, device_id_type=pl.DeviceIdType.MESH)

    greet(mate)
    for entry in direct:

        @pl.when(entry[5])
        def _(entry=entry):
            greet(entry[3])

    pl.semaphore_wait(barrier, 1 + sum(jnp.where(entry[5], 1, 0) for entry in direct))
    for n, source, there, target, here, sends, receives in direct:

        @pl.when(sends)
        def _(n=n, source=source, there=there, target=target):
            copy(n, source, there, target).start()

    first = copy(0, x_ref, 3 - side, mate)
    first.start()
    own = pltpu.make_async_copy(x_ref, out_ref.at[3], local_sem)
    own.start()
    for step in (-3, -2, -1, 1, 2, 3):

        @pl.when(jnp.logical_not(present(me - step)))
        def _(step=step):
            out_ref[3 - step] = jnp.zeros(x_ref.shape, x_ref.dtype)

    own.wait()
    first.wait_send()
    copy(0, x_ref, 3 + side, mate).wait_recv()
    for entry, hand in zip(direct[1:], passed):

        @pl.when(entry[6])
        def _(entry=entry, hand=hand):
            copy(entry[0], x_ref, entry[4], entry[3]).wait_recv()
            copy(hand[0], hand[1], hand[2], mate).start()

    for n, source, there, target, here, sends, receives in direct + passed:

        @pl.when(sends)
        def _(n=n, source=source, there=there, target=target):
            copy(n, source, there, target).wait_send()

    for n, source, there, target, here, sends, receives in direct[:1] + passed:

        @pl.when(receives)
        def _(n=n, here=here, target=target):
            copy(n, x_ref, here, target).wait_recv()


def relay(x, identity):
    return pl.pallas_call(
        relay_kernel,
        in_specs=[pl.BlockSpec(memory_space=pltpu.VMEM)],
        out_specs=pl.BlockSpec(memory_space=pltpu.VMEM),
        out_shape=jax.ShapeDtypeStruct((7,) + x.shape, x.dtype),
        scratch_shapes=[
            pltpu.SemaphoreType.DMA((6,)),
            pltpu.SemaphoreType.DMA((6,)),
            pltpu.SemaphoreType.DMA,
        ],
        compiler_params=pltpu.CompilerParams(
            collective_id=identity, has_side_effects=True, vmem_limit_bytes=24 * 2**20
        ),
    )(x)


def shared_gather(block):
    core = lax.axis_index("seq") % 2
    half = block.shape[0] // 2
    mine = lax.dynamic_slice_in_dim(block, core * half, half, 0)
    mine = lax.all_gather(mine, "batch", axis=0, tiled=False)
    other = lax.ppermute(mine, "seq", [(i, i ^ 1) for i in range(lax.axis_size("seq"))])
    even = core == 0
    return jnp.concatenate([jnp.where(even, mine, other), jnp.where(even, other, mine)], axis=1)


def gather_ring(block, dim):
    devices = lax.axis_size("batch")
    me = lax.axis_index("batch")
    width = block.shape[dim]
    shape = list(block.shape)
    shape[dim] = devices * width
    total = jnp.zeros(shape, block.dtype)
    for step in range(devices):
        piece = block
        if step:
            piece = lax.ppermute(block, "batch", [(b, (b + step) % devices) for b in range(devices)])
        total = lax.dynamic_update_slice_in_dim(total, piece, (me - step) % devices * width, dim)
    return total


def dot(a, b):
    return jnp.dot(a, b, preferred_element_type=F32)


def norm_rows(values, gain):
    scaled = values * lax.rsqrt(jnp.mean(values * values, axis=-1, keepdims=True) + 1e-06)
    return (scaled * gain).astype(BF16)


def unit_heads(p):
    a = lax.broadcasted_iota(jnp.int32, (SLAB, SLAB), 0) // HEAD
    b = lax.broadcasted_iota(jnp.int32, (SLAB, SLAB), 1) // HEAD
    ones = (a == b).astype(F32).astype(BF16)
    parts = []
    for g in range(D // SLAB):
        piece = p[:, g * SLAB : (g + 1) * SLAB]
        square = piece * piece
        high = square.astype(BF16)
        low = (square - high.astype(F32)).astype(BF16)
        total = dot(high, ones) + dot(low, ones)
        scale = lax.rsqrt(total * (1.0 / HEAD) + 1e-06) * (1.0 / HEAD**0.5)
        parts.append((piece * scale).astype(BF16))
    return jnp.concatenate(parts, axis=1)


def dense0_kernel(own, codes_ref, high_ref, low_ref, table_ref, gain_ref, w_ref, k_ref, v_ref, q_ref, mixed_ref):
    vocab = lax.broadcasted_iota(jnp.int32, (VOCAB, TILE), 0)
    hot = [
        (codes_ref[j : j + 1, :] == vocab).astype(F32).astype(BF16) for j in range(KERNEL)
    ]
    dims = (((0,), (0,)), ((), ()))
    stream = lax.dot_general(hot[KERNEL // 2], table_ref[...], dims, preferred_element_type=F32)
    every = jnp.concatenate(hot, axis=0)
    conv = lax.dot_general(every, high_ref[...], dims, preferred_element_type=F32)
    conv += lax.dot_general(every, low_ref[...], dims, preferred_element_type=F32)
    mixed = (stream + conv / (1.0 + jnp.exp(-conv))).astype(BF16)
    inputs = norm_rows(mixed.astype(F32), gain_ref[...])
    k_ref[...] = unit_heads(dot(inputs, w_ref[:, D : 2 * D]))
    v_ref[...] = dot(inputs, w_ref[:, 2 * D :]).astype(BF16)

    @pl.when(pl.program_id(0) == own)
    def _():
        q_ref[...] = unit_heads(dot(inputs, w_ref[:, :D]))
        mixed_ref[...] = mixed


def dense0(codes9, high, low, table, gain, w, own):
    rows = codes9.shape[1]
    whole = lambda shape: pl.BlockSpec(shape, lambda i: (0, 0))
    tile = pl.BlockSpec((TILE, D), lambda i: (i, 0))
    return pl.pallas_call(
        lambda *refs: dense0_kernel(own, *refs),
        grid=(rows // TILE,),
        in_specs=[
            pl.BlockSpec((codes9.shape[0], TILE), lambda i: (0, i)),
            whole(high.shape),
            whole(low.shape),
            whole(table.shape),
            whole(gain.shape),
            whole(w.shape),
        ],
        out_specs=[tile, tile, whole((TILE, D)), whole((TILE, D))],
        out_shape=[jax.ShapeDtypeStruct((rows, D), BF16)] * 2
        + [jax.ShapeDtypeStruct((TILE, D), BF16)] * 2,
        compiler_params=pltpu.CompilerParams(vmem_limit_bytes=40 * 2**20),
        cost_estimate=pl.CostEstimate(
            flops=2 * rows * D * (3 * D), bytes_accessed=4 * rows * D + 2**21, transcendentals=rows * D
        ),
    )(codes9, high, low, table, gain, w)


def project_kernel(own, x_ref, w_ref, k_ref, v_ref, q_ref):
    inputs = x_ref[...]
    k_ref[...] = unit_heads(dot(inputs, w_ref[:, D : 2 * D]))
    v_ref[...] = dot(inputs, w_ref[:, 2 * D :]).astype(BF16)

    @pl.when(pl.program_id(0) == own)
    def _():
        q_ref[...] = unit_heads(dot(inputs, w_ref[:, :D]))


def project(x, w, own):
    rows = x.shape[0]
    whole = lambda shape: pl.BlockSpec(shape, lambda i: (0, 0))
    tile = pl.BlockSpec((TILE, D), lambda i: (i, 0))
    return pl.pallas_call(
        lambda *refs: project_kernel(own, *refs),
        grid=(rows // TILE,),
        in_specs=[tile, whole(w.shape)],
        out_specs=[tile, tile, whole((TILE, D))],
        out_shape=[jax.ShapeDtypeStruct((rows, D), BF16)] * 2
        + [jax.ShapeDtypeStruct((TILE, D), BF16)],
        compiler_params=pltpu.CompilerParams(vmem_limit_bytes=40 * 2**20),
        cost_estimate=pl.CostEstimate(
            flops=2 * rows * D * (2 * D), bytes_accessed=6 * rows * D + 2**21, transcendentals=rows * D
        ),
    )(x, w)


def attention_kernel(
    list_ref, count_ref, mult_ref, q_ref, k_ref, v_ref, mixed_ref, w_ref, out_ref, s_ref, m_ref, l_ref, acc_ref
):
    i = pl.program_id(0)
    count = count_ref[i]
    pairs = (count + 1) // 2
    lane = lax.broadcasted_iota(jnp.int32, (BLK, SLAB), 1) // HEAD
    joined = []

    def chunk(ref, p, g):
        first = pl.multiple_of(list_ref[i, 2 * p] * BLK, BLK)
        second = pl.multiple_of(list_ref[i, 2 * p + 1] * BLK, BLK)
        lanes = slice(g * SLAB, (g + 1) * SLAB)
        return jnp.concatenate([ref[pl.ds(first, BLK), lanes], ref[pl.ds(second, BLK), lanes]], axis=0)

    def gathered(ref, base, blocks, g):
        lanes = slice(g * SLAB, (g + 1) * SLAB)
        starts = [pl.multiple_of(list_ref[i, base + n] * BLK, BLK) for n in range(blocks)]
        return jnp.concatenate([ref[pl.ds(start, BLK), lanes] for start in starts], axis=0)

    for g in range(HEADS // GROUP):
        q = q_ref[:, g * SLAB : (g + 1) * SLAB]
        stacked = jnp.concatenate(
            [jnp.where(lane == h, q, jnp.zeros_like(q)) for h in range(GROUP)], axis=0
        )
        l_ref[...] = jnp.zeros_like(l_ref)
        acc_ref[...] = jnp.zeros_like(acc_ref)
        mults = [mult_ref[g * GROUP + h] for h in range(GROUP)]
        narrow = jnp.maximum(jnp.maximum(mults[0], mults[1]), jnp.maximum(mults[2], mults[3])) <= NARROW

        @pl.when(narrow)
        def _(g=g, stacked=stacked, mults=mults):
            def step(base, blocks, masked):
                keys, values = gathered(k_ref, base, blocks, g), gathered(v_ref, base, blocks, g)
                s = lax.dot_general(stacked, keys, (((1,), (1,)), ((), ())), preferred_element_type=F32)
                probs = []
                for h in range(GROUP):
                    rows = slice(h * BLK, (h + 1) * BLK)
                    scaled = s[rows] * mults[h]
                    if masked:
                        bias = jnp.where(base + 1 < count, 0.0, -1e30).astype(F32)
                        scaled = jnp.concatenate([scaled[:, :BLK], scaled[:, BLK:] + bias], axis=1)
                    expo = jnp.exp2(scaled)
                    part = expo[:, :BLK]
                    for n in range(1, blocks):
                        part += expo[:, n * BLK : (n + 1) * BLK]
                    l_ref[rows, :] += part
                    probs.append(expo.astype(BF16))
                acc_ref[...] += dot(jnp.concatenate(probs, axis=0), values)

            quads = count // 4
            lax.fori_loop(0, quads, lambda p, c: (step(4 * p, 4, False), c)[1], 0)
            rest = (count - 4 * quads + 1) // 2
            lax.fori_loop(0, rest, lambda p, c: (step(4 * quads + 2 * p, 2, True), c)[1], 0)

        @pl.when(jnp.logical_not(narrow))
        def _(g=g, stacked=stacked):
            m_ref[...] = jnp.full_like(m_ref, -1e30)

            def score(p, carry):
                s = lax.dot_general(
                    stacked, chunk(k_ref, p, g), (((1,), (1,)), ((), ())), preferred_element_type=F32
                )
                bias = jnp.where(2 * p + 1 < count, 0.0, -1e30).astype(F32)
                left, right = s[:, :BLK], s[:, BLK:] + bias
                s_ref[p, :, :BLK] = left
                s_ref[p, :, BLK:] = right
                m_ref[...] = jnp.maximum(m_ref[...], jnp.maximum(left, right))
                return carry

            lax.fori_loop(0, pairs, score, 0)
            for h in range(GROUP):
                rows = slice(h * BLK, (h + 1) * BLK)
                peak = jnp.max(m_ref[rows, :], axis=1, keepdims=True) * mult_ref[g * GROUP + h]
                m_ref[rows, :] = jnp.broadcast_to(peak, (BLK, BLK))

            def weigh(p, carry):
                probs = []
                for h in range(GROUP):
                    rows = slice(h * BLK, (h + 1) * BLK)
                    mult = mult_ref[g * GROUP + h]
                    peak = m_ref[rows, :]
                    left = jnp.exp2(s_ref[p, rows, :BLK] * mult - peak)
                    right = jnp.exp2(s_ref[p, rows, BLK:] * mult - peak)
                    l_ref[rows, :] += left + right
                    probs.append(jnp.concatenate([left.astype(BF16), right.astype(BF16)], axis=1))
                acc_ref[...] += dot(jnp.concatenate(probs, axis=0), chunk(v_ref, p, g))
                return carry

            lax.fori_loop(0, pairs, weigh, 0)
        result = jnp.zeros((BLK, SLAB), F32)
        for h in range(GROUP):
            rows = slice(h * BLK, (h + 1) * BLK)
            total = jnp.sum(l_ref[rows, :], axis=1, keepdims=True)
            result = jnp.where(lane == h, acc_ref[rows, :] * (1.0 / total), result)
        joined.append(result.astype(BF16))
    update = dot(jnp.concatenate(joined, axis=1), w_ref[...])
    out_ref[...] = (mixed_ref[...].astype(F32) + update).astype(BF16)


def attention(lists, counts, mult, q, k, v, mixed, w):
    rows = q.shape[0]
    whole = lambda shape: pl.BlockSpec(shape, lambda i, *_: (0, 0))
    tile = pl.BlockSpec((BLK, D), lambda i, *_: (i, 0))
    half = (2 * WIN + 2) // 2
    return pl.pallas_call(
        attention_kernel,
        grid_spec=pltpu.PrefetchScalarGridSpec(
            num_scalar_prefetch=3,
            grid=(rows // BLK,),
            in_specs=[tile, whole(k.shape), whole(v.shape), tile, whole(w.shape)],
            out_specs=tile,
            scratch_shapes=[
                pltpu.VMEM((half, GROUP * BLK, 2 * BLK), F32),
                pltpu.VMEM((GROUP * BLK, BLK), F32),
                pltpu.VMEM((GROUP * BLK, BLK), F32),
                pltpu.VMEM((GROUP * BLK, SLAB), F32),
            ],
        ),
        out_shape=jax.ShapeDtypeStruct((rows, D), BF16),
        compiler_params=pltpu.CompilerParams(vmem_limit_bytes=48 * 2**20),
        cost_estimate=pl.CostEstimate(
            flops=16 * 10**9, bytes_accessed=8 * 2**20, transcendentals=rows * HEADS * 13 * BLK
        ),
    )(lists, counts, mult, q, k, v, mixed, w)


def tap_products(table, gain, taps):
    held = taps.shape[0]
    devices = lax.axis_size("batch")
    me = lax.axis_index("batch")
    spans = [(-(-(b + 1) * held // D)) - b * held // D for b in range(devices)]
    span = min(KERNEL, max(spans))

    def first(b):
        return jnp.minimum(b * held // D, KERNEL - span)

    normed = norm_rows(table.astype(F32), gain)
    begin = me * held
    copies = -(-held // D) + 1
    columns = lax.dynamic_slice_in_dim(jnp.tile(normed, (1, copies)), begin % D, held, 1)
    tap = (begin + jnp.arange(held, dtype=jnp.int32)) // D - first(me)
    mask = tap[None, :] == jnp.arange(span, dtype=jnp.int32)[:, None]
    spread = jnp.where(mask[:, None, :], columns[None], jnp.zeros((), BF16)).reshape(span * VOCAB, held)
    part = dot(spread, taps)
    total = jnp.zeros((KERNEL * VOCAB, D), F32)
    for step in range(devices):
        if step == 0:
            piece = part
        else:
            piece = lax.ppermute(part, "batch", [(b, (b + step) % devices) for b in range(devices)])
        place = first((me - step) % devices) * VOCAB
        total += lax.dynamic_update_slice_in_dim(jnp.zeros_like(total), piece, place, 0)
    return total


def local(codes, table, gains, taps, qkv, mixing, divisors, permitted):
    rows = codes.shape[1]
    rims = -(-WIN * BLK // rows)
    blocks = rows // BLK
    first_block = lax.axis_index("seq") * blocks
    total_blocks = blocks * lax.axis_size("seq")

    offsets = jnp.arange(-WIN, WIN + 1, dtype=jnp.int32)
    index = jnp.arange(blocks, dtype=jnp.int32)[:, None]
    target = first_block + index + offsets[None, :]
    allowed = (target >= 0) & (target < total_blocks)
    allowed = allowed[None] & ((permitted == 1) | (offsets == 0)[None, None])
    counts = jnp.sum(allowed.astype(jnp.int32), axis=-1)
    order = jnp.arange(2 * WIN + 1)
    place = jnp.sum(
        (allowed[:, :, None, :] & (order[None, :] < order[:, None])[None, None]).astype(jnp.int32), axis=-1
    )
    slots = jnp.arange(2 * WIN + 2, dtype=jnp.int32)
    picked = allowed[:, :, None, :] & (place[:, :, None, :] == slots[None, None, :, None])
    window = index + offsets[None, :] + rims * blocks
    lists = jnp.sum(jnp.where(picked, window[None, :, None, :], 0), axis=-1)
    mult = divisors * LOG2E

    wide = exchange(codes[0].reshape(-1, BLK) + 1, rims + 1, 0).reshape(-1) - 1
    begin = rows - KERNEL // 2
    span = (2 * rims + 1) * rows
    codes9 = jnp.stack([wide[begin + j : begin + j + span] for j in range(KERNEL)] + [wide[:span]] * (16 - KERNEL))
    products = tap_products(table, gains[0, 0], taps[0])
    high = products.astype(BF16)
    low = (products - high.astype(F32)).astype(BF16)
    outs = gather_ring(mixing, 1)
    w0 = shared_gather(qkv[0]).transpose(1, 0, 2).reshape(D, 3 * D)
    k, v, q, mixed = dense0(codes9, high, low, table, gains[0, 1][None], w0, rims)
    taps1 = shared_gather(taps[1]).reshape(KERNEL * D, D)
    late, mixed = lax.optimization_barrier((qkv[1], mixed))
    w1 = lax.all_gather(late, "batch", axis=1, tiled=True)
    stream = attention(lists[0], counts[0], mult[0], q, k, v, mixed, outs[0])

    half = KERNEL // 2
    normed = norm_rows(stream.astype(F32), gains[1, 0])
    edges = exchange(jnp.concatenate([normed[:8], normed[rows - 8 :]], axis=0), 1, 1)
    padded = jnp.concatenate([edges[0, 16 - half :], normed, edges[2, :half]], axis=0)
    unfold = jnp.concatenate([padded[j : j + rows] for j in range(KERNEL)], axis=1)
    conv = dot(unfold, taps1)
    mixed = (stream.astype(F32) + jax.nn.silu(conv)).astype(BF16)
    inputs = norm_rows(mixed.astype(F32), gains[1, 1])
    k, v, q = project((relay(inputs, 2) if rims == 3 else exchange(inputs, rims, 2)).reshape(-1, D), w1, rims)
    return attention(lists[1], counts[1], mult[1], q, k, v, mixed, outs[1])[None]


def solution(mesh):
    in_specs = (
        P("batch", "seq"),
        P(),
        P(),
        P(None, "batch", None),
        P(None, None, "batch"),
        P(None, "batch", None),
        P(),
        P(None, "seq", None),
    )
    out_specs = P("batch", "seq", None)
    return jax.shard_map(local, mesh=mesh, in_specs=in_specs, out_specs=out_specs, check_vma=False)
```
